32 devices in a mesh: batch: 16 (over z, x, core), tensor: 2 (over y).
Axes of the slice: x: 2, y: 2, z: 4, core: 2. Of those that a mesh axis runs over, the one named last changes fastest.
Arguments:
- tokens: bfloat16 [9216, 768], P('batch'), may hold values from -6 to 6
- doc_vectors: bfloat16 [32, 768], P('batch'), may hold values from -3 to 3
- doc_ids: int32 [32], P('batch'), may hold values from 0 to 31, as said below
- w_query: bfloat16 [768, 768], P(None, 'tensor'), may hold values from -0.21875 to 0.21875
- b_query: bfloat16 [768], P('tensor'), may hold values from -2 to 2
- w_key: bfloat16 [768, 768], P(None, 'tensor'), may hold values from -0.21875 to 0.21875
- w_value: bfloat16 [768, 768], P(None, 'tensor'), may hold values from -0.21875 to 0.21875
- b_value: bfloat16 [768], P('tensor'), may hold values from -2 to 2
- w_out: bfloat16 [768, 768], P('tensor'), may hold values from -1.25 to 1.25
- b_out: bfloat16 [768], replicated, may hold values from -2 to 2
- gain_one: bfloat16 [768], replicated, may hold values from 0.25 to 1.75
- shift_one: bfloat16 [768], replicated, may hold values from -2 to 2
- w_inner: bfloat16 [768, 3072], P(None, 'tensor'), may hold values from -0.21875 to 0.21875
- b_inner: bfloat16 [3072], P('tensor'), may hold values from -2 to 2
- w_outer: bfloat16 [3072, 768], P('tensor'), may hold values from -0.109375 to 0.109375
- b_outer: bfloat16 [768], replicated, may hold values from -2 to 2
- gain_two: bfloat16 [768], replicated, may hold values from 0.25 to 1.75
- shift_two: bfloat16 [768], replicated, may hold values from -2 to 2
- cotangent: bfloat16 [9216, 768], P('batch'), may hold values from -6 to 6
Outputs:
- mixed: bfloat16 [9216, 768], P('batch')
- tokens_grad: bfloat16 [9216, 768], P('batch')
- doc_grad: float32 [32, 768], P('batch')
- w_query_grad: float32 [768, 768], P('batch', 'tensor')
- b_query_grad: float32 [768], P(('tensor', 'batch'))
- w_key_grad: float32 [768, 768], P('batch', 'tensor')
- w_value_grad: float32 [768, 768], P('batch', 'tensor')
- b_value_grad: float32 [768], P(('tensor', 'batch'))
- w_out_grad: float32 [768, 768], P('tensor', 'batch')
- b_out_grad: float32 [768], P('batch')
- gain_one_grad: float32 [768], P('batch')
- shift_one_grad: float32 [768], P('batch')
- w_inner_grad: float32 [768, 3072], P('batch', 'tensor')
- b_inner_grad: float32 [3072], P(('tensor', 'batch'))
- w_outer_grad: float32 [3072, 768], P('tensor', 'batch')
- b_outer_grad: float32 [768], P('batch')
- gain_two_grad: float32 [768], P('batch')
- shift_two_grad: float32 [768], P('batch')
The draws below stay inside these ranges and needn't reach their ends.
Inputs may be any that keep to these rules, and one draw needn't show every extreme that they name: `doc_ids`: the first pair on every index of batch names one common document; the last pair names document 32 - 1.
All inputs are finite; a program needn't handle non-finite values.
Results may differ from the reference program's by a relative error of at most 0.017.
The reference program's roundings to bfloat16 on the way count: a program that leaves them out, or rounds other values in their place, can miss the bound.
Values may be sent and summed in bfloat16 or wider, within the bound.
A program may use at most 128 MiB of HBM per device.

```python
import jax
import jax.numpy as jnp
from jax import lax

D = 768
HEADS = 12
HEAD_DIM = 64
FF = 3072
SEQ = 288
QLEN = 32
PAIRS_DEV = 2
PAIRS = 32
TOKENS = 9216
NDOCS = 32
N_BATCH = 16


def draw_doc_ids(key, part):
    key = jax.random.fold_in(key, 11)
    key_random, key_common = jax.random.split(key)
    chosen = jax.random.randint(key_random, (PAIRS,), 0, NDOCS)
    common = jax.random.randint(key_common, (), 0, NDOCS)
    places = jnp.arange(PAIRS)
    chosen = jnp.where(places % PAIRS_DEV == 0, common, chosen)
    chosen = jnp.where(places == PAIRS - 1, NDOCS - 1, chosen)
    return chosen.astype(jnp.int32)


def strengthened(result, own_key, source, target, parts, factor):
    def block_of(position):
        return (jnp.arange(result.shape[position]) // (result.shape[position] // parts)).reshape((-1,) + (1,) * (result.ndim - 1 - position))

    near = jax.random.permutation(own_key, parts)[block_of(target)]
    other_side = (block_of(target) + parts // 2) % parts
    return jnp.where((block_of(source) == near) | (block_of(source) == other_side), factor * result, result)


def steps_of(stream_key, shape, shards, smallest, high):
    factor_of = 1.0
    for dim, parts in shards:
        draws = jax.random.uniform(jax.random.fold_in(jax.random.fold_in(stream_key, 6), dim), (parts,), jnp.float32, smallest / len(shards), high / len(shards))
        factor_of = factor_of * jnp.repeat(jnp.exp(draws), shape[dim] // parts).reshape((-1,) + (1,) * (len(shape) - 1 - dim))
    return factor_of


def gaussian(own_key, shape, scale, reach, shards=(), held_as=jnp.bfloat16):
    drawn = scale * jax.random.normal(own_key, shape, jnp.float32)
    if shards:
        drawn = drawn * steps_of(own_key, shape, shards, -0.22, 0.18)
    return jnp.clip(drawn, -reach, reach).astype(held_as)


def noise_with(own_key, shape, width, bound, pieces, heavy, dtype=jnp.bfloat16):
    result = width * jax.random.normal(own_key, shape, jnp.float32)
    if pieces:
        result = result * steps_of(own_key, shape, pieces, -0.22, 0.18)
    return jnp.clip(strengthened(result, jax.random.fold_in(own_key, 3), *heavy), -bound, bound).astype(dtype)


def setup_inputs(seed: int = 0) -> dict:
    key_of = jax.random.split(jax.random.key(seed), 20)
    return {
        "tokens": noise_with(key_of[0], (TOKENS, D), 1.0, 6.0, ((0, 16),), (0, 1, 16, 2.0)),
        "doc_vectors": gaussian(key_of[1], (NDOCS, D), 0.5, 3.0, ((0, 16),)),
        "doc_ids": draw_doc_ids(jax.random.fold_in(key_of[19], 71), 0),
        "w_query": gaussian(key_of[3], (D, D), D ** -0.5, 0.21875, ((1, 2),)),
        "b_query": gaussian(key_of[4], (D,), 0.3, 2.0, ((0, 2),)),
        "w_key": gaussian(key_of[5], (D, D), D ** -0.5, 0.21875, ((1, 2),)),
        "w_value": gaussian(key_of[6], (D, D), D ** -0.5, 0.21875, ((1, 2),)),
        "b_value": gaussian(key_of[7], (D,), 0.3, 2.0, ((0, 2),)),
        "w_out": gaussian(key_of[8], (D, D), (D // 32) ** -0.5, 1.25, ((0, 2),)),
        "b_out": gaussian(key_of[9], (D,), 0.3, 2.0),
        "gain_one": jnp.clip(1.0 + 0.15 * jax.random.normal(key_of[10], (D,), jnp.float32), 0.25, 1.75).astype(jnp.bfloat16),
        "shift_one": gaussian(key_of[11], (D,), 0.3, 2.0),
        "w_inner": gaussian(key_of[12], (D, FF), D ** -0.5, 0.21875, ((1, 2),)),
        "b_inner": gaussian(key_of[13], (FF,), 0.3, 2.0, ((0, 2),)),
        "w_outer": gaussian(key_of[14], (FF, D), FF ** -0.5, 0.109375, ((0, 2),)),
        "b_outer": gaussian(key_of[15], (D,), 0.3, 2.0),
        "gain_two": jnp.clip(1.0 + 0.15 * jax.random.normal(key_of[16], (D,), jnp.float32), 0.25, 1.75).astype(jnp.bfloat16),
        "shift_two": gaussian(key_of[17], (D,), 0.3, 2.0),
        "cotangent": noise_with(key_of[18], (TOKENS, D), 1.0, 6.0, ((0, 16),), (0, 1, 16, 2.0)),
    }


@jax.custom_vjp
def low(v):
    return lax.optimization_barrier(v.astype(jnp.bfloat16)).astype(jnp.float32)

@jax.custom_vjp
def low_back(v):
    return v

def low_keep(v):
    return (low(v), None)

def low_pass(kept, grad):
    return (grad,)

def back_keep(v):
    return (v, None)

def back_low(kept, grad):
    return (low(grad),)
low.defvjp(low_keep, low_pass)
low_back.defvjp(back_keep, back_low)
highest = lax.Precision.HIGHEST
epsilon = 1e-12

def matmul(left, right):
    return jnp.dot(left, right, precision=highest)

def layer_norm(summed, gain, shift):
    centre = lax.optimization_barrier(jnp.mean(summed, axis=-1, keepdims=True))
    centered = summed - centre
    inverse = lax.rsqrt(lax.optimization_barrier(jnp.mean(centered * centered, axis=-1, keepdims=True)) + epsilon)
    return centered * inverse * gain + shift

def forward(token_rows, pair_docs, doc_table, w_query, b_query, w_key, w_value, b_value, w_out, b_out, gain_one, shift_one, w_inner, b_inner, w_outer, b_outer, gain_two, shift_two):
    group_pairs = pair_docs.shape[0]
    seq_len = token_rows.shape[0] // group_pairs
    chosen = doc_table[pair_docs]
    doc_mask = (jnp.arange(seq_len) >= QLEN).astype(jnp.float32)
    inputs = (token_rows.reshape(group_pairs, seq_len, D) + doc_mask[None, :, None] * chosen[:, None, :]).reshape(-1, D)
    low_inputs = low(inputs)
    shape_heads = (group_pairs, seq_len, HEADS, HEAD_DIM)
    queries = low(low_back(matmul(low_inputs, w_query) + b_query)).reshape(shape_heads)
    keys = low(low_back(matmul(low_inputs, w_key))).reshape(shape_heads)
    values = low(low_back(matmul(low_inputs, w_value) + b_value)).reshape(shape_heads)
    scores = low_back(jnp.einsum('gqhe,gkhe->ghqk', queries, keys, precision=highest) * HEAD_DIM ** (-0.5))
    row_max = lax.optimization_barrier(jnp.max(scores, axis=-1, keepdims=True))
    weights = jnp.exp(scores - row_max)
    probs = weights / lax.optimization_barrier(jnp.sum(weights, axis=-1, keepdims=True))
    attended = jnp.einsum('ghqk,gkhe->gqhe', low(probs), values, precision=highest)
    attended = low(low_back(attended.reshape(-1, D)))
    attn_out = low_back(matmul(attended, w_out)) + b_out
    hidden_one = layer_norm(inputs + attn_out, gain_one, shift_one)
    inner = low_back(matmul(low(hidden_one), w_inner) + b_inner)
    activated = low(jax.nn.gelu(inner, approximate=False))
    outer = low_back(matmul(activated, w_outer)) + b_outer
    return layer_norm(hidden_one + outer, gain_two, shift_two)

def reference(tokens, doc_vectors, doc_ids, w_query, b_query, w_key, w_value, b_value, w_out, b_out, gain_one, shift_one, w_inner, b_inner, w_outer, b_outer, gain_two, shift_two, cotangent):
    params = tuple((item.astype(jnp.float32) for item in (doc_vectors, w_query, b_query, w_key, w_value, b_value, w_out, b_out, gain_one, shift_one, w_inner, b_inner, w_outer, b_outer, gain_two, shift_two)))
    group_rows = PAIRS_DEV * SEQ
    token_groups = tokens.astype(jnp.float32).reshape(N_BATCH, group_rows, D)
    cot_groups = cotangent.astype(jnp.float32).reshape(N_BATCH, group_rows, D)
    id_groups = doc_ids.astype(jnp.int32).reshape(N_BATCH, PAIRS_DEV)

    def group_step(totals, inputs):
        token_block, cot_block, id_block = inputs

        def local(token_values, weights_all):
            return forward(token_values, id_block, *weights_all)
        output, pull = jax.vjp(local, token_block, params)
        token_grad, param_grads = pull(cot_block)
        totals = tuple((running + fresh for running, fresh in zip(totals, param_grads)))
        return (totals, (output.astype(jnp.bfloat16), token_grad.astype(jnp.bfloat16)))
    zeros = tuple((jnp.zeros_like(item) for item in params))
    totals, (outputs, token_grads) = lax.scan(group_step, zeros, (token_groups, cot_groups, id_groups))
    return (outputs.reshape(TOKENS, D), token_grads.reshape(TOKENS, D), totals[0], totals[1], totals[2], totals[3], totals[4], totals[5], totals[6], totals[7], totals[8], totals[9], totals[10], totals[11], totals[12], totals[13], totals[14], totals[15])
```

```python
import functools
import math

import jax
import jax.numpy as jnp
from jax import lax
from jax.experimental import pallas as pl
from jax.experimental.pallas import tpu as pltpu
from jax.sharding import PartitionSpec as P

HEAD_DIM = 64
QLEN = 32
LANES = 128
GROUP = 16
EPSILON = 1e-12
F32 = jnp.float32
BF16 = jnp.bfloat16
MESH = pl.DeviceIdType.MESH

ROW_BQ, ROW_BV, ROW_BOUT, ROW_G1, ROW_S1, ROW_BIN, ROW_BOUTER, ROW_G2, ROW_S2 = range(9)
SMALL_ROWS = 16


def product(left, right, left_dim=1, right_dim=0):
    return lax.dot_general(
        left, right, (((left_dim,), (right_dim,)), ((), ())), preferred_element_type=F32
    )


def fold_rows(block):
    return jnp.sum(block.reshape(block.shape[0] // 8, 8, block.shape[1]), axis=0)


def row_mean(block):
    return jnp.mean(block, axis=1, keepdims=True)


def layer_kernel(
    sizes,
    tokens_hbm, cot_hbm, wq_hbm, wk_hbm, wv_hbm, wo_hbm, wi_hbm, w2_hbm,
    docs_ref, ids_ref, bq_ref, bv_ref, bo_ref, g1_ref, s1_ref, bi_ref, b2_ref, g2_ref, s2_ref,
    mixed_hbm, tgrad_hbm, grads_out, small_out, docs_out,
    tok, cot, wq, wk, wv, wo, wi, w2,
    x_low, q_s, k_s, v_s, p_s, att, n1_s, r1_s, h1_low, g_s, sl_s, dz_s, df_s, du_s,
    da_s, dq_s, dk_s, dv_s, out_s, acc, accb, accq, bin_s,
    y_send, y_recv, sb, rb0, rb1, rb2, ss, rs0, rs1, rs2,
    doc_stage, doc_table, doc_part, doc_in,
    y_ssem, y_rsem, r_ssem, r_rsem, d_ssem, d_rsem, load_sem, out_sem,
):
    n_batch, pairs, seq = sizes
    rows, width = tok.shape
    local = wq.shape[1]
    hidden = wi.shape[1]
    chunk = width // GROUP
    docs_dev = docs_ref.shape[0]
    doc_cols = width // LANES
    inner = n_batch // GROUP

    b = lax.axis_index("batch")
    t = lax.axis_index("tensor")
    place = b // inner
    rest = b % inner
    core = place % 2
    xpos = (place // 2) % 2
    zpos = place // 4
    zs = GROUP // 4

    def at_place(other):
        return (other * inner + rest, t)

    y_peer = (b, 1 - t)
    core_peer = at_place(place + 1 - 2 * core)
    x_peer = at_place(place + 2 - 4 * xpos)

    def z_peer(step):
        return at_place(((zpos + step) % zs) * 4 + xpos * 2 + core)

    def batch_peer(step):
        return ((b + step) % n_batch, t)

    loads = []
    for i, (src, dst) in enumerate(
        (
            (tokens_hbm, tok), (wq_hbm, wq), (wk_hbm, wk), (wv_hbm, wv),
            (wo_hbm, wo), (wi_hbm, wi), (w2_hbm, w2), (cot_hbm, cot),
        )
    ):
        copy = pltpu.make_async_copy(src, dst, load_sem.at[i])
        copy.start()
        loads.append(copy)
    (tok_load, wq_load, wk_load, wv_load, wo_load, wi_load, w2_load, cot_load) = loads

    barrier = pltpu.get_barrier_semaphore()

    def greet(step, carry):
        pl.semaphore_signal(barrier, inc=1, device_id=batch_peer(step), device_id_type=MESH)
        return carry

    lax.fori_loop(1, n_batch, greet, 0)
    pl.semaphore_signal(barrier, inc=1, device_id=y_peer, device_id_type=MESH)

    doc_rows = docs_ref[...].astype(F32)
    pieces = []
    for n in range(docs_dev):
        for j in range(8):
            if j < doc_cols:
                pieces.append(doc_rows[n : n + 1, j * LANES : (j + 1) * LANES])
            else:
                pieces.append(jnp.zeros((1, LANES), F32))
    stage = jnp.concatenate(pieces, axis=0).astype(BF16)
    doc_stage[...] = stage
    doc_table[b] = stage

    bq = bq_ref[...].astype(F32).reshape(1, local)
    bv = bv_ref[...].astype(F32).reshape(1, local)
    b_out = bo_ref[...].astype(F32).reshape(1, width)
    gain1 = g1_ref[...].astype(F32).reshape(1, width)
    shift1 = s1_ref[...].astype(F32).reshape(1, width)
    bin_s[...] = bi_ref[...].astype(F32).reshape(1, hidden)
    b_outer = b2_ref[...].astype(F32).reshape(1, width)
    gain2 = g2_ref[...].astype(F32).reshape(1, width)
    shift2 = s2_ref[...].astype(F32).reshape(1, width)

    pl.semaphore_wait(barrier, n_batch)

    def doc_copy(step):
        return pltpu.make_async_remote_copy(
            src_ref=doc_stage,
            dst_ref=doc_table.at[b],
            send_sem=d_ssem.at[0, step],
            recv_sem=d_rsem.at[0, b],
            device_id=batch_peer(step),
            device_id_type=MESH,
        )

    def doc_arrival(step):
        other = (b + step) % n_batch
        return pltpu.make_async_remote_copy(
            src_ref=doc_stage,
            dst_ref=doc_table.at[other],
            send_sem=d_ssem.at[0, step],
            recv_sem=d_rsem.at[0, other],
            device_id=batch_peer(step),
            device_id_type=MESH,
        )

    def doc_start(step, carry):
        doc_copy(step).start()
        return carry

    def doc_wait(step, carry):
        doc_arrival(step).wait_recv()
        return carry

    def doc_sent(step, carry):
        doc_copy(step).wait_send()
        return carry

    lax.fori_loop(1, n_batch, doc_start, 0)
    tok_load.wait()
    lax.fori_loop(1, n_batch, doc_wait, 0)

    ids = [jnp.full((8, LANES), ids_ref[p], jnp.int32) for p in range(pairs)]

    def pick(d, found):
        block = doc_table[d].astype(F32)
        result = []
        for p in range(pairs):
            value = found[p]
            for n in range(docs_dev):
                value = value + jnp.where(
                    ids[p] == d * docs_dev + n, block[8 * n : 8 * n + 8, :], 0.0
                )
            result.append(value)
        return tuple(result)

    found = lax.fori_loop(
        0, n_batch, pick, tuple(jnp.zeros((8, LANES), F32) for _ in range(pairs))
    )
    doc_row = [
        jnp.concatenate([found[p][j : j + 1, :] for j in range(doc_cols)], axis=1)
        for p in range(pairs)
    ]

    def pair_rows(p):
        return pl.ds(p * seq, seq)

    def blocks(size):
        return seq // size

    def inputs_of(p, i, size):
        base = pl.multiple_of(i * size, size)
        where_row = base + lax.broadcasted_iota(jnp.int32, (size, 1), 0)
        rows_here = pl.ds(pl.multiple_of(p * seq + i * size, 16), size)
        values = tok[rows_here, :].astype(F32) + jnp.where(where_row >= QLEN, doc_row[p], 0.0)
        return rows_here, values

    def y_copy(kind, p):
        return pltpu.make_async_remote_copy(
            src_ref=y_send.at[kind, p],
            dst_ref=y_recv.at[kind, p],
            send_sem=y_ssem.at[kind, p],
            recv_sem=y_rsem.at[kind, p],
            device_id=y_peer,
            device_id_type=MESH,
        )

    def y_sum(kind, p, i, size):
        here = pl.ds(pl.multiple_of(i * size, 16), size)
        return y_send[kind, p, here, :].astype(F32) + y_recv[kind, p, here, :].astype(F32)

    O_SUM, F_SUM, DH_SUM, DX_SUM = range(4)
    first_lanes = lax.broadcasted_iota(jnp.int32, (1, LANES), 1) < HEAD_DIM

    def head_lanes(values, h):
        keep = first_lanes if h == 0 else jnp.logical_not(first_lanes)
        return jnp.where(keep, values, jnp.zeros_like(values))

    def add_acc(which, p, value):
        if p == 0:
            acc[which] = value
        else:
            acc[which] = acc[which] + value

    A_G2, A_S2, A_BOUTER, A_G1, A_S1, A_BOUT = range(6)

    BLOCK = 96

    def make_inputs(p):
        @pl.loop(0, blocks(BLOCK))
        def _(i):
            rows_here, values = inputs_of(p, i, BLOCK)
            x_low[rows_here, :] = values.astype(BF16)

    def attention(p):
        mine = pair_rows(p)
        xl = x_low[mine, :]
        q_s[mine, :] = ((product(xl, wq[...]) + bq).astype(BF16).astype(F32) * 0.125).astype(BF16)
        k_s[mine, :] = product(xl, wk[...]).astype(BF16)
        v_s[mine, :] = (product(xl, wv[...]) + bv).astype(BF16)

        @pl.loop(0, local // LANES)
        def _(j):
            cols = pl.ds(pl.multiple_of(j * LANES, LANES), LANES)
            qq, kk, vv = q_s[mine, cols], k_s[mine, cols], v_s[mine, cols]
            outs = []
            for h in range(2):
                scores = product(head_lanes(qq, h), kk, 1, 1)
                expo = jnp.exp(scores - jnp.max(scores, axis=1, keepdims=True))
                probs = expo * (1.0 / jnp.sum(expo, axis=1, keepdims=True))
                p_s[p * (local // HEAD_DIM) + 2 * j + h] = probs
                outs.append(product(probs.astype(BF16), vv))
            att[mine, cols] = jnp.where(first_lanes, outs[0], outs[1]).astype(BF16)

    def attention_out(p):
        y_send[O_SUM, p] = product(att[pair_rows(p), :], wo[...]).astype(BF16)

    def norm_one(p):
        @pl.loop(0, blocks(BLOCK))
        def _(i):
            rows_here, values = inputs_of(p, i, BLOCK)
            summed = values + (y_sum(O_SUM, p, i, BLOCK) + b_out)
            centered = summed - row_mean(summed)
            inverse = lax.rsqrt(row_mean(centered * centered) + EPSILON)
            normed = centered * inverse
            n1_s[rows_here, :] = normed
            r1_s[rows_here, :] = inverse
            h1_low[rows_here, :] = (normed * gain1 + shift1).astype(BF16)

    FF_TILE = 512

    def feed_forward(p):
        mine = pair_rows(p)

        @pl.loop(0, hidden // FF_TILE)
        def _(j):
            cols = pl.ds(pl.multiple_of(j * FF_TILE, LANES), FF_TILE)
            u = product(h1_low[mine, :], wi[:, cols]) + bin_s[:, cols]
            cdf = 0.5 * (1.0 + lax.erf(u * (1.0 / math.sqrt(2.0))))
            density = jnp.exp(-0.5 * u * u) * (1.0 / math.sqrt(2.0 * math.pi))
            g_s[mine, cols] = (u * cdf).astype(BF16)
            sl_s[mine, cols] = cdf + u * density

        half = width // 2

        @pl.loop(0, 2)
        def _(j):
            cols = pl.ds(pl.multiple_of(j * half, LANES), half)
            y_send[F_SUM, p, :, cols] = product(g_s[mine, :], w2[:, cols]).astype(BF16)

    def norm_two(p):
        def step(i, sums):
            size = BLOCK
            here = pl.ds(pl.multiple_of(p * seq + i * size, 16), size)
            h1 = n1_s[here, :] * gain1 + shift1
            summed = h1 + (y_sum(F_SUM, p, i, size) + b_outer)
            centered = summed - row_mean(summed)
            inverse = lax.rsqrt(row_mean(centered * centered) + EPSILON)
            normed = centered * inverse
            out_s[here, :] = (normed * gain2 + shift2).astype(BF16)
            dy = cot[here, :].astype(F32)
            dyn = dy * normed
            scaled = dy * gain2
            dz = inverse * (scaled - row_mean(scaled) - normed * row_mean(scaled * normed))
            dz_s[here, :] = dz
            df_s[here, :] = dz.astype(BF16)
            return (sums[0] + fold_rows(dyn), sums[1] + fold_rows(dy), sums[2] + fold_rows(dz))

        zero = jnp.zeros((8, width), F32)
        sums = lax.fori_loop(0, blocks(BLOCK), step, (zero, zero, zero))
        add_acc(A_G2, p, sums[0])
        add_acc(A_S2, p, sums[1])
        add_acc(A_BOUTER, p, sums[2])

    def feed_forward_back(p):
        mine = pair_rows(p)

        @pl.loop(0, hidden // FF_TILE)
        def _(j):
            cols = pl.ds(pl.multiple_of(j * FF_TILE, LANES), FF_TILE)
            da = product(df_s[mine, :], w2[cols, :], 1, 1)
            du = (da * sl_s[mine, cols]).astype(BF16)
            du_s[mine, cols] = du
            total = fold_rows(du.astype(F32))
            if p == 0:
                accb[:, cols] = total
            else:
                accb[:, cols] = accb[:, cols] + total

        third = width // 3

        @pl.loop(0, 3)
        def _(j):
            cols = pl.ds(pl.multiple_of(j * third, LANES), third)
            y_send[DH_SUM, p, :, cols] = product(du_s[mine, :], wi[cols, :], 1, 1).astype(BF16)

    def norm_one_back(p):
        def step(i, sums):
            size = BLOCK
            here = pl.ds(pl.multiple_of(p * seq + i * size, 16), size)
            dh = dz_s[here, :] + y_sum(DH_SUM, p, i, size)
            normed = n1_s[here, :]
            scaled = dh * gain1
            dz = r1_s[here, :] * (
                scaled - row_mean(scaled) - normed * row_mean(scaled * normed)
            )
            dz_s[here, :] = dz
            df_s[here, :] = dz.astype(BF16)
            return (
                sums[0] + fold_rows(dh * normed),
                sums[1] + fold_rows(dh),
                sums[2] + fold_rows(dz),
            )

        zero = jnp.zeros((8, width), F32)
        sums = lax.fori_loop(0, blocks(BLOCK), step, (zero, zero, zero))
        add_acc(A_G1, p, sums[0])
        add_acc(A_S1, p, sums[1])
        add_acc(A_BOUT, p, sums[2])

    def attention_back(p):
        mine = pair_rows(p)
        da_s[mine, :] = product(df_s[mine, :], wo[...], 1, 1).astype(BF16)

        @pl.loop(0, local // LANES)
        def _(j):
            cols = pl.ds(pl.multiple_of(j * LANES, LANES), LANES)
            qq, kk, vv, dd = q_s[mine, cols], k_s[mine, cols], v_s[mine, cols], da_s[mine, cols]
            dqs, dks, dvs = [], [], []
            for h in range(2):
                probs = p_s[p * (local // HEAD_DIM) + 2 * j + h]
                dvs.append(product(probs.astype(BF16), dd, 0, 0))
                dp = product(head_lanes(dd, h), vv, 1, 1)
                ds = probs * (dp - jnp.sum(probs * dp, axis=1, keepdims=True))
                ds = ds.astype(BF16)
                dqs.append(product(ds, kk))
                dks.append(product(ds, qq, 0, 0))
            dq_s[mine, cols] = (jnp.where(first_lanes, dqs[0], dqs[1]) * 0.125).astype(BF16)
            dk_s[mine, cols] = jnp.where(first_lanes, dks[0], dks[1]).astype(BF16)
            dv_s[mine, cols] = jnp.where(first_lanes, dvs[0], dvs[1]).astype(BF16)

        total_q = fold_rows(dq_s[mine, :].astype(F32))
        total_v = fold_rows(dv_s[mine, :].astype(F32))
        if p == 0:
            accq[0] = total_q
            accq[1] = total_v
        else:
            accq[0] = accq[0] + total_q
            accq[1] = accq[1] + total_v

    def inputs_back(p):
        mine = pair_rows(p)
        third = width // 3

        @pl.loop(0, 3)
        def _(j):
            cols = pl.ds(pl.multiple_of(j * third, LANES), third)
            y_send[DX_SUM, p, :, cols] = (
                product(dq_s[mine, :], wq[cols, :], 1, 1)
                + product(dk_s[mine, :], wk[cols, :], 1, 1)
                + product(dv_s[mine, :], wv[cols, :], 1, 1)
            ).astype(BF16)

    def weight_grad(m, left, right, first, tile):
        @pl.loop(0, right.shape[1] // tile)
        def _(j):
            cols = pl.ds(pl.multiple_of(j * tile, LANES), tile)
            out_cols = pl.ds(pl.multiple_of(first + j * tile, LANES), tile)
            grad = product(left[...], right[:, cols], 0, 0)
            for r in range(GROUP):
                sb[m, r % 2, (r // 2) % 2, r // 4, :, out_cols] = grad[
                    r * chunk : (r + 1) * chunk, :
                ].astype(BF16)

    def reduce_refs(m):
        if m < 3:
            return sb.at[m], rb0.at[m], rb1.at[m], rb2.at[m]
        return ss, rs0, rs1, rs2

    def core_copy(m):
        mine, r0, _, _ = reduce_refs(m)
        return pltpu.make_async_remote_copy(
            src_ref=mine.at[1 - core],
            dst_ref=r0,
            send_sem=r_ssem.at[m, 0],
            recv_sem=r_rsem.at[m, 0],
            device_id=core_peer,
            device_id_type=MESH,
        )

    def x_copy(m):
        mine, _, r1, _ = reduce_refs(m)
        return pltpu.make_async_remote_copy(
            src_ref=mine.at[core, 1 - xpos],
            dst_ref=r1,
            send_sem=r_ssem.at[m, 1],
            recv_sem=r_rsem.at[m, 1],
            device_id=x_peer,
            device_id_type=MESH,
        )

    def z_copy(m, step):
        mine, _, _, r2 = reduce_refs(m)
        return pltpu.make_async_remote_copy(
            src_ref=mine.at[core, xpos, (zpos + step) % zs],
            dst_ref=r2.at[step - 1],
            send_sem=r_ssem.at[m, 1 + step],
            recv_sem=r_rsem.at[m, 1 + step],
            device_id=z_peer(step),
            device_id_type=MESH,
        )

    def add_into(mine, index, other):
        for zz in range(zs):
            value = mine[(*index, zz)].astype(F32) + other[zz].astype(F32)
            mine[(*index, zz)] = value.astype(mine.dtype)

    def reduce_x(m):
        mine, r0, _, _ = reduce_refs(m)
        core_copy(m).wait_recv()
        add_into(mine, (core, 1 - xpos), r0.at[1 - xpos])
        x_copy(m).start()
        add_into(mine, (core, xpos), r0.at[xpos])

    def reduce_z(m):
        mine, _, r1, _ = reduce_refs(m)
        x_copy(m).wait_recv()
        add_into(mine, (core, xpos), r1)
        for step in range(1, zs):
            z_copy(m, step).start()

    def reduce_end(m):
        mine, _, _, r2 = reduce_refs(m)
        total = mine[core, xpos, zpos].astype(F32)
        for step in range(1, zs):
            z_copy(m, step).wait_recv()
        for step in range(1, zs):
            total = total + r2[step - 1].astype(F32)
        if m < 3:
            grads_out[m] = total
        else:
            small_out[...] = total

    def reduce_sent(m):
        core_copy(m).wait_send()
        x_copy(m).wait_send()
        for step in range(1, zs):
            z_copy(m, step).wait_send()

    def place_vector(row, eight):
        vector = jnp.sum(eight, axis=0, keepdims=True)
        piece = vector.shape[1] // GROUP
        for r in range(GROUP):
            ss[r % 2, (r // 2) % 2, r // 4, row : row + 1, 0:piece] = vector[
                :, r * piece : (r + 1) * piece
            ]

    for p in range(pairs):
        make_inputs(p)
        if p == 0:
            wq_load.wait()
            wk_load.wait()
            wv_load.wait()
        attention(p)
        if p == 0:
            wo_load.wait()
        attention_out(p)
        y_copy(O_SUM, p).start()
    for p in range(pairs):
        y_copy(O_SUM, p).wait_recv()
        norm_one(p)
        if p == 0:
            wi_load.wait()
            w2_load.wait()
        feed_forward(p)
        y_copy(F_SUM, p).start()
    cot_load.wait()
    ss[...] = jnp.zeros(ss.shape, F32)
    for p in range(pairs):
        y_copy(F_SUM, p).wait_recv()
        norm_two(p)
        if p == pairs - 1:
            weight_grad(0, df_s, g_s, 0, FF_TILE)
            core_copy(0).start()
        feed_forward_back(p)
        y_copy(DH_SUM, p).start()
    mixed_copy = pltpu.make_async_copy(out_s, mixed_hbm, out_sem.at[0])
    mixed_copy.start()
    reduce_x(0)
    weight_grad(1, h1_low, du_s, 0, FF_TILE)
    core_copy(1).start()
    place_vector(ROW_G2, acc[A_G2])
    place_vector(ROW_S2, acc[A_S2])
    place_vector(ROW_BOUTER, acc[A_BOUTER])
    place_vector(ROW_BIN, accb[...])
    reduce_x(1)
    for p in range(pairs):
        y_copy(DH_SUM, p).wait_recv()
        norm_one_back(p)
        attention_back(p)
        inputs_back(p)
        y_copy(DX_SUM, p).start()
        if p == 0:
            reduce_z(0)
    weight_grad(2, df_s, att, 0, local)
    weight_grad(2, x_low, dq_s, local, local)
    weight_grad(2, x_low, dk_s, 2 * local, local)
    weight_grad(2, x_low, dv_s, 3 * local, local)
    core_copy(2).start()
    place_vector(ROW_G1, acc[A_G1])
    place_vector(ROW_S1, acc[A_S1])
    place_vector(ROW_BOUT, acc[A_BOUT])
    place_vector(ROW_BQ, accq[0])
    place_vector(ROW_BV, accq[1])
    core_copy(3).start()
    reduce_z(1)
    reduce_x(2)
    reduce_x(3)
    reduce_end(0)
    mixed_copy.wait()

    sums = []
    for p in range(pairs):
        y_copy(DX_SUM, p).wait_recv()

        def step(i, total, p=p):
            size = 32
            here = pl.ds(pl.multiple_of(p * seq + i * size, 16), size)
            dx = dz_s[here, :] + y_sum(DX_SUM, p, i, size)
            out_s[here, :] = dx.astype(BF16)
            return total + jnp.where(i * size >= QLEN, fold_rows(dx), 0.0)

        total = lax.fori_loop(0, seq // 32, step, jnp.zeros((8, width), F32))
        sums.append(jnp.sum(total, axis=0, keepdims=True))
    tgrad_copy = pltpu.make_async_copy(out_s, tgrad_hbm, out_sem.at[1])
    tgrad_copy.start()

    zero_row = jnp.zeros((1, LANES), F32)
    sum_blocks = [
        jnp.concatenate(
            [sums[p][:, j * LANES : (j + 1) * LANES] for j in range(doc_cols)]
            + [zero_row] * (8 - doc_cols),
            axis=0,
        )
        for p in range(pairs)
    ]

    def fill(d, carry):
        for n in range(docs_dev):
            value = jnp.zeros((8, LANES), F32)
            for p in range(pairs):
                value = value + jnp.where(ids[p] == d * docs_dev + n, sum_blocks[p], 0.0)
            doc_part[d, 8 * n : 8 * n + 8, :] = value
        return carry

    lax.fori_loop(0, n_batch, fill, 0)

    def part_copy(step):
        other = (b + step) % n_batch
        return pltpu.make_async_remote_copy(
            src_ref=doc_part.at[other],
            dst_ref=doc_in.at[b],
            send_sem=d_ssem.at[1, step],
            recv_sem=d_rsem.at[1, b],
            device_id=(other, t),
            device_id_type=MESH,
        )

    def part_arrival(step):
        other = (b + step) % n_batch
        return pltpu.make_async_remote_copy(
            src_ref=doc_part.at[other],
            dst_ref=doc_in.at[other],
            send_sem=d_ssem.at[1, step],
            recv_sem=d_rsem.at[1, other],
            device_id=(other, t),
            device_id_type=MESH,
        )

    def part_start(step, carry):
        part_copy(step).start()
        return carry

    def part_wait(step, carry):
        part_arrival(step).wait_recv()
        return carry

    def part_sent(step, carry):
        part_copy(step).wait_send()
        return carry

    lax.fori_loop(1, n_batch, part_start, 0)
    doc_in[b] = doc_part[b]

    reduce_z(2)
    reduce_z(3)
    reduce_end(1)
    lax.fori_loop(1, n_batch, part_wait, 0)

    def add_part(d, total):
        return total + doc_in[d]

    docs_out[...] = lax.fori_loop(0, n_batch, add_part, jnp.zeros(docs_out.shape, F32))
    reduce_end(2)
    reduce_end(3)

    for kind in range(4):
        for p in range(pairs):
            y_copy(kind, p).wait_send()
    for m in range(4):
        reduce_sent(m)
    lax.fori_loop(1, n_batch, doc_sent, 0)
    lax.fori_loop(1, n_batch, part_sent, 0)
    tgrad_copy.wait()


def finish_kernel(
    local, grads_ref, small_ref, docs_ref,
    doc_out, wq_out, bq_out, wk_out, wv_out, bv_out, wo_out, bo_out, g1_out, s1_out,
    wi_out, bi_out, w2_out, b2_out, g2_out, s2_out,
):
    docs_dev, width = doc_out.shape
    for n in range(docs_dev):
        for j in range(width // LANES):
            doc_out[n : n + 1, j * LANES : (j + 1) * LANES] = docs_ref[8 * n + j : 8 * n + j + 1, :]
    w2_out[...] = grads_ref[0]
    wi_out[...] = grads_ref[1]
    wo_out[...] = grads_ref[2, :, 0:local]
    wq_out[...] = grads_ref[2, :, local : 2 * local]
    wk_out[...] = grads_ref[2, :, 2 * local : 3 * local]
    wv_out[...] = grads_ref[2, :, 3 * local : 4 * local]
    for row, out in (
        (ROW_BQ, bq_out), (ROW_BV, bv_out), (ROW_BOUT, bo_out), (ROW_G1, g1_out),
        (ROW_S1, s1_out), (ROW_BIN, bi_out), (ROW_BOUTER, b2_out), (ROW_G2, g2_out),
        (ROW_S2, s2_out),
    ):
        out[...] = small_ref[row, 0 : out.shape[0]]


def body(
    n_batch,
    tokens, doc_vectors, doc_ids, w_query, b_query, w_key, w_value, b_value, w_out, b_out,
    gain_one, shift_one, w_inner, b_inner, w_outer, b_outer, gain_two, shift_two, cotangent,
):
    rows, width = tokens.shape
    pairs = doc_ids.shape[0]
    seq = rows // pairs
    local = w_query.shape[1]
    heads = local // HEAD_DIM
    hidden = w_inner.shape[1]
    docs_dev = doc_vectors.shape[0]
    chunk = width // GROUP
    zs = GROUP // 4
    hbm = pl.BlockSpec(memory_space=pl.ANY)
    vmem = pl.BlockSpec(memory_space=pltpu.VMEM)
    smem = pl.BlockSpec(memory_space=pltpu.SMEM)
    V = pltpu.VMEM
    dma = pltpu.SemaphoreType.DMA
    scratch = [
        V((rows, width), BF16), V((rows, width), BF16),
        V((width, local), BF16), V((width, local), BF16), V((width, local), BF16),
        V((local, width), BF16), V((width, hidden), BF16), V((hidden, width), BF16),
        V((rows, width), BF16),
        V((rows, local), BF16), V((rows, local), BF16), V((rows, local), BF16),
        V((pairs * heads, seq, seq), F32),
        V((rows, local), BF16),
        V((rows, width), F32), V((rows, 1), F32), V((rows, width), BF16),
        V((rows, hidden), BF16), V((rows, hidden), F32),
        V((rows, width), F32), V((rows, width), BF16), V((rows, hidden), BF16),
        V((rows, local), BF16), V((rows, local), BF16), V((rows, local), BF16),
        V((rows, local), BF16),
        V((rows, width), BF16),
        V((6, 8, width), F32), V((8, hidden), F32), V((2, 8, local), F32), V((1, hidden), F32),
        V((4, pairs, seq, width), BF16), V((4, pairs, seq, width), BF16),
        V((3, 2, 2, zs, chunk, hidden), BF16), V((3, 2, zs, chunk, hidden), BF16),
        V((3, zs, chunk, hidden), BF16), V((3, zs - 1, chunk, hidden), BF16),
        V((2, 2, zs, SMALL_ROWS, LANES), F32), V((2, zs, SMALL_ROWS, LANES), F32),
        V((zs, SMALL_ROWS, LANES), F32), V((zs - 1, SMALL_ROWS, LANES), F32),
        V((8 * docs_dev, LANES), BF16), V((n_batch, 8 * docs_dev, LANES), BF16),
        V((n_batch, 8 * docs_dev, LANES), F32), V((n_batch, 8 * docs_dev, LANES), F32),
        dma((4, pairs)), dma((4, pairs)), dma((4, zs + 1)), dma((4, zs + 1)),
        dma((2, n_batch)), dma((2, n_batch)), dma((8,)), dma((2,)),
    ]
    shape = jax.ShapeDtypeStruct
    mixed, tokens_grad, grads, small, docs = pl.pallas_call(
        functools.partial(layer_kernel, (n_batch, pairs, seq)),
        out_shape=(
            shape((rows, width), BF16),
            shape((rows, width), BF16),
            shape((3, chunk, hidden), F32),
            shape((SMALL_ROWS, LANES), F32),
            shape((8 * docs_dev, LANES), F32),
        ),
        in_specs=[hbm] * 8 + [vmem, smem] + [vmem] * 9,
        out_specs=(hbm, hbm, vmem, vmem, vmem),
        scratch_shapes=scratch,
        compiler_params=pltpu.CompilerParams(
            collective_id=0, has_side_effects=True, vmem_limit_bytes=60 * 1024 * 1024
        ),
        name="encoder_layer",
    )(
        tokens, cotangent, w_query, w_key, w_value, w_out, w_inner, w_outer,
        doc_vectors, doc_ids, b_query, b_value, b_out, gain_one, shift_one, b_inner, b_outer,
        gain_two, shift_two,
    )

    inner = n_batch // GROUP
    if inner > 1:
        groups = [[g * inner + i for i in range(inner)] for g in range(GROUP)]
        grads = lax.psum_scatter(
            grads, "batch", scatter_dimension=1, axis_index_groups=groups, tiled=True
        )
        small = lax.psum(small, "batch", axis_index_groups=groups)
        part = lax.axis_index("batch") % inner
        pieces = []
        for row in range(SMALL_ROWS):
            wide = {ROW_BQ: local, ROW_BV: local, ROW_BIN: hidden}.get(row, width)
            size = wide // n_batch
            piece = lax.dynamic_slice(small[row], (part * size,), (size,))
            pieces.append(jnp.pad(piece, (0, LANES - size)))
        small = jnp.stack(pieces)

    out_rows = width // n_batch
    vector = shape((out_rows,), F32)
    vector_local = shape((local // n_batch,), F32)
    square = shape((out_rows, local), F32)
    (
        doc_grad, wq_grad, bq_grad, wk_grad, wv_grad, bv_grad, wo_grad, bo_grad, g1_grad, s1_grad,
        wi_grad, bi_grad, w2_grad, b2_grad, g2_grad, s2_grad,
    ) = pl.pallas_call(
        functools.partial(finish_kernel, local),
        out_shape=(
            shape((docs_dev, width), F32), square, vector_local, square, square, vector_local,
            square, vector, vector, vector,
            shape((out_rows, hidden), F32), shape((hidden // n_batch,), F32),
            shape((out_rows, hidden), F32), vector, vector, vector,
        ),
        in_specs=[vmem] * 3,
        out_specs=(vmem,) * 16,
        name="gradient_outputs",
    )(grads, small, docs)
    return (
        mixed, tokens_grad, doc_grad, wq_grad, bq_grad, wk_grad, wv_grad, bv_grad, wo_grad.T,
        bo_grad, g1_grad, s1_grad, wi_grad, bi_grad, w2_grad.T, b2_grad, g2_grad, s2_grad,
    )


def solution(mesh):
    in_specs = (
        P("batch", None), P("batch", None), P("batch"), P(None, "tensor"), P("tensor"),
        P(None, "tensor"), P(None, "tensor"), P("tensor"), P("tensor", None), P(), P(), P(),
        P(None, "tensor"), P("tensor"), P("tensor", None), P(), P(), P(), P("batch", None),
    )
    out_specs = (
        P("batch", None), P("batch", None), P("batch", None), P("batch", "tensor"),
        P(("tensor", "batch")), P("batch", "tensor"), P("batch", "tensor"),
        P(("tensor", "batch")), P("tensor", "batch"), P("batch"), P("batch"), P("batch"),
        P("batch", "tensor"), P(("tensor", "batch")), P("tensor", "batch"), P("batch"),
        P("batch"), P("batch"),
    )
    return jax.shard_map(
        functools.partial(body, mesh.shape["batch"]),
        mesh=mesh, in_specs=in_specs, out_specs=out_specs, check_vma=False,
    )
```

```python
import functools
import math

import jax
import jax.numpy as jnp
from jax import lax
from jax.experimental import pallas as pl
from jax.experimental.pallas import tpu as pltpu
from jax.sharding import PartitionSpec as P

HEAD_DIM = 64
QLEN = 32
LANES = 128
GROUP = 16
EPSILON = 1e-12
F32 = jnp.float32
BF16 = jnp.bfloat16
MESH = pl.DeviceIdType.MESH

ROW_BQ, ROW_BV, ROW_BOUT, ROW_G1, ROW_S1, ROW_BIN, ROW_BOUTER, ROW_G2, ROW_S2 = range(9)
SMALL_ROWS = 16


def product(left, right, left_dim=1, right_dim=0):
    return lax.dot_general(
        left, right, (((left_dim,), (right_dim,)), ((), ())), preferred_element_type=F32
    )


def fold_rows(block):
    return jnp.sum(block.reshape(block.shape[0] // 8, 8, block.shape[1]), axis=0)


def row_mean(block):
    return jnp.mean(block, axis=1, keepdims=True)


def layer_kernel(
    sizes,
    tokens_hbm, cot_hbm, wq_hbm, wk_hbm, wv_hbm, wo_hbm, wi_hbm, w2_hbm,
    docs_ref, ids_ref, bq_ref, bv_ref, bo_ref, g1_ref, s1_ref, bi_ref, b2_ref, g2_ref, s2_ref,
    mixed_hbm, tgrad_hbm, grads_out, small_out, docs_out,
    tok, cot, w_qkv, wo_all, wi, w2,
    x_low, qkv_s, p_s, att_all, n1_s, r1_s, h1_low, g_s, sl_s, dz_s, df_s, du_s,
    da_s, dqkv_s, out_s, acc, accb, accq, accx,
    y_send, y_recv, ff0, ff1, ff2, ff3, ff4, at0, at1, at2, at3, at4, ss0, ss1, ss2, ss3, ss4,
    doc_stage, doc_table, doc_part, doc_in, sum_send, sum_recv,
    y_ssem, y_rsem, a_ssem, a_rsem, w_ssem, w_rsem, r_ssem, r_rsem, d_ssem, d_rsem,
    s_ssem, s_rsem, load_sem, out_sem,
):
    n_batch, pairs, seq = sizes
    rows, width = tok.shape
    local = wq_hbm.shape[1]
    hidden = wi.shape[1]
    chunk = width // GROUP
    docs_dev = docs_ref.shape[0]
    doc_cols = width // LANES
    inner = n_batch // GROUP

    b = lax.axis_index("batch")
    t = lax.axis_index("tensor")
    place = b // inner
    rest = b % inner
    core = place % 2
    xpos = (place // 2) % 2
    zlow = (place // 4) % 2
    zhigh = place // 8

    def at_place(other):
        return (other * inner + rest, t)

    y_peer = (b, 1 - t)
    core_peer = at_place(place + 1 - 2 * core)
    x_peer = at_place(place + 2 - 4 * xpos)
    zlow_peer = at_place(place + 4 - 8 * zlow)
    zhigh_peer = at_place(place + 8 - 16 * zhigh)

    def batch_peer(step):
        return ((b + step) % n_batch, t)

    wo_mine = pl.ds(pl.multiple_of(t * local, LANES), local)
    att_mine = wo_mine
    loads = []
    for i, (src, dst) in enumerate(
        (
            (tokens_hbm, tok), (wq_hbm, w_qkv.at[:, 0:local]),
            (wk_hbm, w_qkv.at[:, local : 2 * local]), (wv_hbm, w_qkv.at[:, 2 * local :]),
            (wo_hbm, wo_all.at[wo_mine]), (wi_hbm, wi), (w2_hbm, w2), (cot_hbm, cot),
        )
    ):
        copy = pltpu.make_async_copy(src, dst, load_sem.at[i])
        copy.start()
        loads.append(copy)
    (tok_load, wq_load, wk_load, wv_load, wo_load, wi_load, w2_load, cot_load) = loads

    barrier = pltpu.get_barrier_semaphore()

    def greet(step, carry):
        pl.semaphore_signal(barrier, inc=1, device_id=batch_peer(step), device_id_type=MESH)
        return carry

    lax.fori_loop(1, n_batch, greet, 0)
    pl.semaphore_signal(barrier, inc=1, device_id=y_peer, device_id_type=MESH)

    doc_rows = docs_ref[...].astype(F32)
    pieces = []
    for n in range(docs_dev):
        for j in range(8):
            if j < doc_cols:
                pieces.append(doc_rows[n : n + 1, j * LANES : (j + 1) * LANES])
            else:
                pieces.append(jnp.zeros((1, LANES), F32))
    stage = jnp.concatenate(pieces, axis=0).astype(BF16)
    doc_stage[...] = stage
    doc_table[b] = stage

    b_qkv = jnp.concatenate(
        [
            bq_ref[...].astype(F32).reshape(1, local),
            jnp.zeros((1, local), F32),
            bv_ref[...].astype(F32).reshape(1, local),
        ],
        axis=1,
    )
    b_out = bo_ref[...].astype(F32).reshape(1, width)
    gain1 = g1_ref[...].astype(F32).reshape(1, width)
    shift1 = s1_ref[...].astype(F32).reshape(1, width)
    b_inner = bi_ref[...].astype(F32).reshape(1, hidden)
    b_outer = b2_ref[...].astype(F32).reshape(1, width)
    gain2 = g2_ref[...].astype(F32).reshape(1, width)
    shift2 = s2_ref[...].astype(F32).reshape(1, width)

    pl.semaphore_wait(barrier, n_batch)

    share = local // 4

    def share_rows(tensor, first, count):
        start = tensor * local + first * share
        return pl.ds(pl.multiple_of(start, 16), count * share)

    quarter = 2 * core + xpos
    out_weight_copies = [
        pltpu.make_async_remote_copy(
            src_ref=source,
            dst_ref=wo_all.at[target],
            send_sem=w_ssem.at[i],
            recv_sem=w_rsem.at[i],
            device_id=peer,
            device_id_type=MESH,
        )
        for i, (source, target, peer) in enumerate(
            (
                (
                    wo_hbm.at[pl.ds(pl.multiple_of(quarter * share, 16), share)],
                    share_rows(t, quarter, 1),
                    y_peer,
                ),
                (
                    wo_all.at[share_rows(1 - t, quarter, 1)],
                    share_rows(1 - t, quarter, 1),
                    x_peer,
                ),
                (
                    wo_all.at[share_rows(1 - t, 2 * core, 2)],
                    share_rows(1 - t, 2 * core, 2),
                    core_peer,
                ),
            )
        )
    ]
    out_weight_copies[0].start()

    def doc_copy(step):
        return pltpu.make_async_remote_copy(
            src_ref=doc_stage,
            dst_ref=doc_table.at[b],
            send_sem=d_ssem.at[0, step],
            recv_sem=d_rsem.at[0, b],
            device_id=batch_peer(step),
            device_id_type=MESH,
        )

    def doc_arrival(step):
        other = (b + step) % n_batch
        return pltpu.make_async_remote_copy(
            src_ref=doc_stage,
            dst_ref=doc_table.at[other],
            send_sem=d_ssem.at[0, step],
            recv_sem=d_rsem.at[0, other],
            device_id=batch_peer(step),
            device_id_type=MESH,
        )

    def doc_start(step, carry):
        doc_copy(step).start()
        return carry

    def doc_wait(step, carry):
        doc_arrival(step).wait_recv()
        return carry

    def doc_sent(step, carry):
        doc_copy(step).wait_send()
        return carry

    lax.fori_loop(1, n_batch, doc_start, 0)

    tok_load.wait()
    lax.fori_loop(1, n_batch, doc_wait, 0)

    ids = [jnp.full((8, LANES), ids_ref[p], jnp.int32) for p in range(pairs)]

    def pick(d, found):
        block = doc_table[d].astype(F32)
        result = []
        for p in range(pairs):
            value = found[p]
            for n in range(docs_dev):
                value = value + jnp.where(
                    ids[p] == d * docs_dev + n, block[8 * n : 8 * n + 8, :], 0.0
                )
            result.append(value)
        return tuple(result)

    found = lax.fori_loop(
        0, n_batch, pick, tuple(jnp.zeros((8, LANES), F32) for _ in range(pairs))
    )
    doc_row = [
        jnp.concatenate([found[p][j : j + 1, :] for j in range(doc_cols)], axis=1)
        for p in range(pairs)
    ]

    def pair_rows(p):
        return pl.ds(p * seq, seq)

    def inputs_of(p):
        where_row = lax.broadcasted_iota(jnp.int32, (seq, 1), 0)
        return tok[pair_rows(p), :].astype(F32) + jnp.where(where_row >= QLEN, doc_row[p], 0.0)

    half = width // 2

    def half_cols(part):
        return pl.ds(part * half, half)

    def y_copy(kind, p, part):
        return pltpu.make_async_remote_copy(
            src_ref=y_send.at[kind, p, :, half_cols(part)],
            dst_ref=y_recv.at[kind, p, :, half_cols(part)],
            send_sem=y_ssem.at[kind, p, part],
            recv_sem=y_rsem.at[kind, p, part],
            device_id=y_peer,
            device_id_type=MESH,
        )

    def y_wait(kind, p):
        for part in range(2):
            y_copy(kind, p, part).wait_recv()

    def y_sum(kind, p):
        return y_send[kind, p].astype(F32) + y_recv[kind, p].astype(F32)

    F_SUM, DH_SUM, DX_SUM = range(3)

    def att_cols(tensor, j):
        return pl.ds(pl.multiple_of(tensor * local + j * LANES, LANES), LANES)

    def att_copy(p, j):
        place_of = att_all.at[pair_rows(p), att_cols(t, j)]
        return pltpu.make_async_remote_copy(
            src_ref=place_of,
            dst_ref=place_of,
            send_sem=a_ssem.at[p, j],
            recv_sem=a_rsem.at[p, j],
            device_id=y_peer,
            device_id_type=MESH,
        )

    first_lanes = lax.broadcasted_iota(jnp.int32, (1, LANES), 1) < HEAD_DIM

    def head_lanes(values, h):
        keep = first_lanes if h == 0 else jnp.logical_not(first_lanes)
        return jnp.where(keep, values, jnp.zeros_like(values))

    def both_heads(values):
        return jnp.concatenate([head_lanes(values, 0), head_lanes(values, 1)], axis=0)

    def add_acc(which, p, value):
        if p == 0:
            acc[which] = value
        else:
            acc[which] = acc[which] + value

    A_G2, A_S2, A_BOUTER, A_G1, A_S1, A_BOUT = range(6)

    def project(p):
        mine = pair_rows(p)
        x_low[mine, :] = inputs_of(p).astype(BF16)
        qkv_s[mine, :] = (product(x_low[mine, :], w_qkv[...]) + b_qkv).astype(BF16)

    def qkv(kind, j):
        return pl.ds(kind * local + j * LANES, LANES)

    def attention(p):
        mine = pair_rows(p)
        for j in range(local // LANES):
            kk, vv = qkv_s[mine, qkv(1, j)], qkv_s[mine, qkv(2, j)]
            qq = (qkv_s[mine, qkv(0, j)].astype(F32) * 0.125).astype(BF16)
            qkv_s[mine, qkv(0, j)] = qq
            low = []
            for h in range(2):
                scores = product(head_lanes(qq, h), kk, 1, 1)
                expo = jnp.exp(scores - jnp.max(scores, axis=1, keepdims=True))
                probs = expo * (1.0 / jnp.sum(expo, axis=1, keepdims=True))
                p_s[p * (local // HEAD_DIM) + 2 * j + h] = probs
                low.append(probs.astype(BF16))
            both = product(low[0], head_lanes(vv, 0)) + product(low[1], head_lanes(vv, 1))
            att_all[mine, att_cols(t, j)] = both.astype(BF16)
            att_copy(p, j).start()

    def attention_out(p):
        for j in range(local // LANES):
            att_copy(p, j).wait_recv()
        mine = pair_rows(p)
        summed = inputs_of(p) + (product(att_all[mine, :], wo_all[...]) + b_out)
        centered = summed - row_mean(summed)
        inverse = lax.rsqrt(row_mean(centered * centered) + EPSILON)
        normed = centered * inverse
        n1_s[mine, :] = normed
        r1_s[mine, :] = inverse
        h1_low[mine, :] = (normed * gain1 + shift1).astype(BF16)

    FF_TILE = 512

    def feed_forward(p):
        mine = pair_rows(p)
        u = product(h1_low[mine, :], wi[...]) + b_inner
        cdf = 0.5 * (1.0 + lax.erf(u * (1.0 / math.sqrt(2.0))))
        density = jnp.exp(-0.5 * u * u) * (1.0 / math.sqrt(2.0 * math.pi))
        g_s[mine, :] = (u * cdf).astype(BF16)
        sl_s[mine, :] = cdf + u * density
        for part in range(2):
            cols = half_cols(part)
            y_send[F_SUM, p, :, cols] = product(g_s[mine, :], w2[:, cols]).astype(BF16)
            y_copy(F_SUM, p, part).start()

    def norm_two(p):
        mine = pair_rows(p)
        h1 = n1_s[mine, :] * gain1 + shift1
        summed = h1 + (y_sum(F_SUM, p) + b_outer)
        centered = summed - row_mean(summed)
        inverse = lax.rsqrt(row_mean(centered * centered) + EPSILON)
        normed = centered * inverse
        out_s[mine, :] = (normed * gain2 + shift2).astype(BF16)
        dy = cot[mine, :].astype(F32)
        scaled = dy * gain2
        dz = inverse * (scaled - row_mean(scaled) - normed * row_mean(scaled * normed))
        dz_s[mine, :] = dz
        df_s[mine, :] = dz.astype(BF16)
        add_acc(A_G2, p, fold_rows(dy * normed))
        add_acc(A_S2, p, fold_rows(dy))
        add_acc(A_BOUTER, p, fold_rows(dz))

    def feed_forward_back(p):
        mine = pair_rows(p)
        du = (product(df_s[mine, :], w2[...], 1, 1) * sl_s[mine, :]).astype(BF16)
        du_s[mine, :] = du
        total = fold_rows(du.astype(F32))
        if p == 0:
            accb[...] = total
        else:
            accb[...] = accb[...] + total
        for part in range(2):
            cols = half_cols(part)
            y_send[DH_SUM, p, :, cols] = product(du_s[mine, :], wi[cols, :], 1, 1).astype(BF16)
            y_copy(DH_SUM, p, part).start()

    def norm_one_back(p):
        mine = pair_rows(p)
        dh = dz_s[mine, :] + y_sum(DH_SUM, p)
        normed = n1_s[mine, :]
        scaled = dh * gain1
        dz = r1_s[mine, :] * (scaled - row_mean(scaled) - normed * row_mean(scaled * normed))
        dz_s[mine, :] = dz
        df_s[mine, :] = dz.astype(BF16)
        doc_part_rows = fold_rows(dz[QLEN:, :])
        accx[p] = doc_part_rows
        add_acc(A_G1, p, fold_rows(dh * normed))
        add_acc(A_S1, p, fold_rows(dh))
        add_acc(A_BOUT, p, doc_part_rows + fold_rows(dz[:QLEN, :]))

    def attention_back(p):
        mine = pair_rows(p)
        da_s[mine, :] = product(df_s[mine, :], wo_all[wo_mine, :], 1, 1).astype(BF16)
        for j in range(local // LANES):
            qq, kk, vv = (qkv_s[mine, qkv(kind, j)] for kind in range(3))
            dd = da_s[mine, pl.ds(j * LANES, LANES)]
            low, ds = [], []
            for h in range(2):
                probs = p_s[p * (local // HEAD_DIM) + 2 * j + h]
                low.append(probs.astype(BF16))
                dp = product(head_lanes(dd, h), vv, 1, 1)
                slope = probs * (dp - jnp.sum(probs * dp, axis=1, keepdims=True))
                ds.append(slope.astype(BF16))
            dv = product(jnp.concatenate(low, axis=0), both_heads(dd), 0, 0)
            dk = product(jnp.concatenate(ds, axis=0), both_heads(qq), 0, 0)
            dq = product(ds[0], head_lanes(kk, 0)) + product(ds[1], head_lanes(kk, 1))
            dqkv_s[mine, qkv(0, j)] = (dq * 0.125).astype(BF16)
            dqkv_s[mine, qkv(1, j)] = dk.astype(BF16)
            dqkv_s[mine, qkv(2, j)] = dv.astype(BF16)
        for i, kind in enumerate((0, 2)):
            total = fold_rows(dqkv_s[mine, pl.ds(kind * local, local)].astype(F32))
            if p == 0:
                accq[i] = total
            else:
                accq[i] = accq[i] + total

    def inputs_back(p):
        mine = pair_rows(p)
        part = product(dqkv_s[mine, :], w_qkv[...], 1, 1)
        y_send[DX_SUM, p] = part.astype(BF16)
        accx[p] = jnp.where(t == 0, accx[p], 0.0) + fold_rows(part[QLEN:, :])

    def inputs_send(p):
        for part in range(2):
            y_copy(DX_SUM, p, part).start()

    N_FF = 6
    N_PIECES = 11
    Z_FIRST = (1, 2, 4)

    def piece_refs(m):
        if m < N_FF:
            return [ref.at[m] for ref in (ff0, ff1, ff2, ff3, ff4)]
        if m < N_PIECES - 1:
            return [ref.at[m - N_FF] for ref in (at0, at1, at2, at3, at4)]
        return [ss0, ss1, ss2, ss3, ss4]

    def chunk_index(m, r):
        low, mid, high, top = r % 2, (r // 2) % 2, (r // 4) % 2, r // 8
        return (low, high, mid, top) if m in Z_FIRST else (low, mid, high, top)

    def my_index(m):
        return (core, zlow, xpos, zhigh) if m in Z_FIRST else (core, xpos, zlow, zhigh)

    def piece_copy(m, phase):
        refs = piece_refs(m)
        index = my_index(m)
        peers = (core_peer, x_peer, zlow_peer, zhigh_peer)
        if m in Z_FIRST:
            peers = (core_peer, zlow_peer, x_peer, zhigh_peer)
        return pltpu.make_async_remote_copy(
            src_ref=refs[0].at[(*index[:phase], 1 - index[phase])],
            dst_ref=refs[phase + 1],
            send_sem=r_ssem.at[m, phase],
            recv_sem=r_rsem.at[m, phase],
            device_id=peers[phase],
            device_id_type=MESH,
        )

    def add_piece(mine, index, other, lead):
        if lead == 0:
            value = mine[index].astype(F32) + other[...].astype(F32)
            mine[index] = value.astype(mine.dtype)
            return
        for k in range(2):
            add_piece(mine, (*index, k), other.at[k], lead - 1)

    def advance(m, phase):
        refs = piece_refs(m)
        index = my_index(m)
        piece_copy(m, phase - 1).wait_recv()
        mine, other = refs[0], refs[phase]
        away, stay = 1 - index[phase], index[phase]
        add_piece(mine, (*index[:phase], away), other.at[away], 3 - phase)
        piece_copy(m, phase).start()
        add_piece(mine, (*index[:phase], stay), other.at[stay], 3 - phase)

    def complete(m):
        refs = piece_refs(m)
        index = my_index(m)
        piece_copy(m, 3).wait_recv()
        total = refs[0][index].astype(F32) + refs[4][...].astype(F32)
        if m < N_FF:
            grads_out[m // 3, :, (m % 3) * FF_TILE : (m % 3 + 1) * FF_TILE] = total
        elif m < N_PIECES - 1:
            n = m - N_FF
            grads_out[2, :, n * local : (n + 1) * local] = total
        else:
            small_out[...] = total

    def weight_grad(m, left, right):
        refs = piece_refs(m)
        grad = product(left, right, 0, 0)
        for r in range(GROUP):
            refs[0][chunk_index(m, r)] = grad[r * chunk : (r + 1) * chunk, :].astype(BF16)
        piece_copy(m, 0).start()

    def outer_grad(n):
        weight_grad(n, df_s[...], g_s[:, n * FF_TILE : (n + 1) * FF_TILE])

    def inner_grad(n):
        weight_grad(3 + n, h1_low[...], du_s[:, n * FF_TILE : (n + 1) * FF_TILE])

    def place_vector(row, eight):
        vector = jnp.sum(eight, axis=0, keepdims=True)
        piece = vector.shape[1] // GROUP
        for r in range(GROUP):
            ss0[(*chunk_index(SMALL, r), slice(row, row + 1), slice(0, piece))] = vector[
                :, r * piece : (r + 1) * piece
            ]

    OUT, QUERY, KEY, VALUE, SMALL = range(N_FF, N_PIECES)

    def qkv_grad(m):
        kind = m - QUERY
        weight_grad(m, x_low[...], dqkv_s[:, kind * local : (kind + 1) * local])

    zero_row = jnp.zeros((1, LANES), F32)
    sum_copy = pltpu.make_async_remote_copy(
        src_ref=sum_send,
        dst_ref=sum_recv,
        send_sem=s_ssem.at[0],
        recv_sem=s_rsem.at[0],
        device_id=y_peer,
        device_id_type=MESH,
    )

    def send_document_sums():
        for p in range(pairs):
            row = jnp.sum(accx[p], axis=0, keepdims=True)
            sum_send[p] = jnp.concatenate(
                [row[:, j * LANES : (j + 1) * LANES] for j in range(doc_cols)]
                + [zero_row] * (8 - doc_cols),
                axis=0,
            )
        sum_copy.start()

    def part_copy(step):
        other = (b + step) % n_batch
        return pltpu.make_async_remote_copy(
            src_ref=doc_part.at[other],
            dst_ref=doc_in.at[b],
            send_sem=d_ssem.at[1, step],
            recv_sem=d_rsem.at[1, b],
            device_id=(other, t),
            device_id_type=MESH,
        )

    def part_arrival(step):
        other = (b + step) % n_batch
        return pltpu.make_async_remote_copy(
            src_ref=doc_part.at[other],
            dst_ref=doc_in.at[other],
            send_sem=d_ssem.at[1, step],
            recv_sem=d_rsem.at[1, other],
            device_id=(other, t),
            device_id_type=MESH,
        )

    def part_start(step, carry):
        part_copy(step).start()
        return carry

    def part_wait(step, carry):
        part_arrival(step).wait_recv()
        return carry

    def part_sent(step, carry):
        part_copy(step).wait_send()
        return carry

    def send_document_parts():
        sum_copy.wait_recv()
        sum_blocks = [sum_send[p] + sum_recv[p] for p in range(pairs)]

        def fill(d, carry):
            for n in range(docs_dev):
                value = jnp.zeros((8, LANES), F32)
                for p in range(pairs):
                    value = value + jnp.where(ids[p] == d * docs_dev + n, sum_blocks[p], 0.0)
                doc_part[d, 8 * n : 8 * n + 8, :] = value
            return carry

        lax.fori_loop(0, n_batch, fill, 0)
        lax.fori_loop(1, n_batch, part_start, 0)
        doc_in[b] = doc_part[b]

    def add_document_parts():
        lax.fori_loop(1, n_batch, part_wait, 0)

        def add_part(d, total):
            return total + doc_in[d]

        docs_out[...] = lax.fori_loop(0, n_batch, add_part, jnp.zeros(docs_out.shape, F32))

    def input_grad(p):
        y_wait(DX_SUM, p)
        out_s[pair_rows(p), :] = (dz_s[pair_rows(p), :] + y_sum(DX_SUM, p)).astype(BF16)
        copy = pltpu.make_async_copy(
            out_s.at[pair_rows(p)], tgrad_hbm.at[pair_rows(p)], out_sem.at[1 + p]
        )
        copy.start()
        return copy

    wq_load.wait()
    wk_load.wait()
    wv_load.wait()
    project(0)
    out_weight_copies[0].wait_recv()
    out_weight_copies[1].start()
    attention(0)
    project(1)
    attention(1)
    out_weight_copies[1].wait_recv()
    out_weight_copies[2].start()
    wo_load.wait()
    out_weight_copies[2].wait_recv()
    wi_load.wait()
    w2_load.wait()
    attention_out(0)
    feed_forward(0)
    attention_out(1)
    feed_forward(1)
    cot_load.wait()
    y_wait(F_SUM, 0)
    norm_two(0)
    feed_forward_back(0)
    y_wait(F_SUM, 1)
    norm_two(1)
    mixed_copy = pltpu.make_async_copy(out_s, mixed_hbm, out_sem.at[0])
    mixed_copy.start()
    outer_grad(1)
    outer_grad(0)
    feed_forward_back(1)
    advance(1, 1)
    inner_grad(1)
    advance(0, 1)
    outer_grad(2)
    inner_grad(2)
    ss0[...] = jnp.zeros(ss0.shape, F32)
    place_vector(ROW_G2, acc[A_G2])
    place_vector(ROW_S2, acc[A_S2])
    place_vector(ROW_BOUTER, acc[A_BOUTER])
    place_vector(ROW_BIN, accb[...])
    inner_grad(0)
    advance(2, 1)
    advance(4, 1)
    advance(5, 1)
    y_wait(DH_SUM, 0)
    norm_one_back(0)
    attention_back(0)
    inputs_back(0)
    inputs_send(0)
    advance(1, 2)
    advance(0, 2)
    advance(3, 1)
    advance(2, 2)
    advance(5, 2)
    advance(1, 3)
    advance(4, 2)
    y_wait(DH_SUM, 1)
    norm_one_back(1)
    weight_grad(OUT, df_s[...], att_all[:, att_mine])
    attention_back(1)
    advance(5, 3)
    qkv_grad(KEY)
    qkv_grad(VALUE)
    advance(OUT, 1)
    complete(1)
    advance(0, 3)
    inputs_back(1)
    send_document_sums()
    inputs_send(1)
    mixed_copy.wait()
    advance(KEY, 1)
    advance(4, 3)
    advance(3, 2)
    complete(5)
    advance(VALUE, 1)
    qkv_grad(QUERY)
    advance(2, 3)
    tgrad_copies = [input_grad(0)]
    place_vector(ROW_G1, acc[A_G1])
    place_vector(ROW_S1, acc[A_S1])
    place_vector(ROW_BOUT, acc[A_BOUT])
    place_vector(ROW_BQ, accq[0])
    place_vector(ROW_BV, accq[1])
    piece_copy(SMALL, 0).start()
    complete(0)
    send_document_parts()
    advance(OUT, 2)
    advance(QUERY, 1)
    advance(SMALL, 1)
    complete(4)
    advance(3, 3)
    advance(KEY, 2)
    add_document_parts()
    complete(2)
    advance(OUT, 3)
    advance(VALUE, 2)
    complete(3)
    advance(KEY, 3)
    tgrad_copies.append(input_grad(1))
    advance(QUERY, 2)
    complete(OUT)
    advance(VALUE, 3)
    advance(SMALL, 2)
    complete(KEY)
    advance(QUERY, 3)
    advance(SMALL, 3)
    complete(VALUE)
    complete(QUERY)
    complete(SMALL)
    for copy in out_weight_copies:
        copy.wait_send()
    sum_copy.wait_send()
    for p in range(pairs):
        for j in range(local // LANES):
            att_copy(p, j).wait_send()
        for kind in range(3):
            for part in range(2):
                y_copy(kind, p, part).wait_send()
    for m in range(N_PIECES):
        for phase in range(4):
            piece_copy(m, phase).wait_send()
    lax.fori_loop(1, n_batch, doc_sent, 0)
    lax.fori_loop(1, n_batch, part_sent, 0)
    for copy in tgrad_copies:
        copy.wait()


def finish_kernel(
    local, mixed_ref, tgrad_ref, grads_ref, small_ref, docs_ref,
    mixed_out, tgrad_out, doc_out, wq_out, bq_out, wk_out, wv_out, bv_out, wo_out, bo_out,
    g1_out, s1_out, wi_out, bi_out, w2_out, b2_out, g2_out, s2_out,
    rows_held, grads_held, in_sem, out_sem,
):
    half = mixed_ref.shape[0] // 2
    moves = []
    for i, (source, target) in enumerate(((mixed_ref, mixed_out), (tgrad_ref, tgrad_out))):
        for k in range(2):
            part = pl.ds(k * half, half)
            moves.append((source.at[part], rows_held.at[i, part], [(rows_held.at[i, part], target.at[part])]))
    for m, targets in enumerate(((w2_out,), (wi_out,), (wo_out, wq_out, wk_out, wv_out))):
        stores = [
            (grads_held.at[m, :, pl.ds(n * local, local)] if m == 2 else grads_held.at[m], target)
            for n, target in enumerate(targets)
        ]
        moves.append((grads_ref.at[m], grads_held.at[m], stores))
    loads = [
        pltpu.make_async_copy(source, held, in_sem.at[i])
        for i, (source, held, _) in enumerate(moves)
    ]
    for copy in loads:
        copy.start()
    docs_dev, width = doc_out.shape
    for n in range(docs_dev):
        for j in range(width // LANES):
            doc_out[n : n + 1, j * LANES : (j + 1) * LANES] = docs_ref[8 * n + j : 8 * n + j + 1, :]
    for row, out in (
        (ROW_BQ, bq_out), (ROW_BV, bv_out), (ROW_BOUT, bo_out), (ROW_G1, g1_out),
        (ROW_S1, s1_out), (ROW_BIN, bi_out), (ROW_BOUTER, b2_out), (ROW_G2, g2_out),
        (ROW_S2, s2_out),
    ):
        out[...] = small_ref[row, 0 : out.shape[0]]
    stored = []
    for copy, (_, _, stores) in zip(loads, moves):
        copy.wait()
        for source, target in stores:
            stored.append(pltpu.make_async_copy(source, target, out_sem.at[len(stored)]))
            stored[-1].start()
    for copy in stored:
        copy.wait()


def body(
    n_batch,
    tokens, doc_vectors, doc_ids, w_query, b_query, w_key, w_value, b_value, w_out, b_out,
    gain_one, shift_one, w_inner, b_inner, w_outer, b_outer, gain_two, shift_two, cotangent,
):
    rows, width = tokens.shape
    pairs = doc_ids.shape[0]
    seq = rows // pairs
    local = w_query.shape[1]
    heads = local // HEAD_DIM
    hidden = w_inner.shape[1]
    docs_dev = doc_vectors.shape[0]
    chunk = width // GROUP
    part = hidden // 3
    hbm = pl.BlockSpec(memory_space=pl.ANY)
    vmem = pl.BlockSpec(memory_space=pltpu.VMEM)
    smem = pl.BlockSpec(memory_space=pltpu.SMEM)
    V = pltpu.VMEM
    dma = pltpu.SemaphoreType.DMA
    scratch = [
        V((rows, width), BF16), V((rows, width), BF16),
        V((width, 3 * local), BF16), V((width, width), BF16), V((width, hidden), BF16), V((hidden, width), BF16),
        V((rows, width), BF16),
        V((rows, 3 * local), BF16),
        V((pairs * heads, seq, seq), F32),
        V((rows, width), BF16),
        V((rows, width), F32), V((rows, 1), F32), V((rows, width), BF16),
        V((rows, hidden), BF16), V((rows, hidden), F32),
        V((rows, width), F32), V((rows, width), BF16), V((rows, hidden), BF16),
        V((rows, local), BF16), V((rows, 3 * local), BF16),
        V((rows, width), BF16),
        V((6, 8, width), F32), V((8, hidden), F32), V((2, 8, local), F32),
        V((pairs, 8, width), F32),
        V((3, pairs, seq, width), BF16), V((3, pairs, seq, width), BF16),
        *[V((6, *(2,) * n, chunk, part), BF16) for n in (4, 3, 2, 1, 0)],
        *[V((4, *(2,) * n, chunk, local), BF16) for n in (4, 3, 2, 1, 0)],
        *[V((*(2,) * n, SMALL_ROWS, LANES), F32) for n in (4, 3, 2, 1, 0)],
        V((8 * docs_dev, LANES), BF16), V((n_batch, 8 * docs_dev, LANES), BF16),
        V((n_batch, 8 * docs_dev, LANES), F32), V((n_batch, 8 * docs_dev, LANES), F32),
        V((pairs, 8, LANES), F32), V((pairs, 8, LANES), F32),
        dma((3, pairs, 2)), dma((3, pairs, 2)), dma((pairs, local // LANES)),
        dma((pairs, local // LANES)), dma((3,)), dma((3,)), dma((11, 4)), dma((11, 4)),
        dma((2, n_batch)), dma((2, n_batch)), dma((1,)), dma((1,)), dma((8,)), dma((1 + pairs,)),
    ]
    shape = jax.ShapeDtypeStruct
    mixed, tokens_grad, grads, small, docs = pl.pallas_call(
        functools.partial(layer_kernel, (n_batch, pairs, seq)),
        out_shape=(
            shape((rows, width), BF16),
            shape((rows, width), BF16),
            shape((3, chunk, hidden), F32),
            shape((SMALL_ROWS, LANES), F32),
            shape((8 * docs_dev, LANES), F32),
        ),
        in_specs=[hbm] * 8 + [vmem, smem] + [vmem] * 9,
        out_specs=(hbm, hbm, vmem, vmem, vmem),
        scratch_shapes=scratch,
        compiler_params=pltpu.CompilerParams(
            collective_id=0, has_side_effects=True, vmem_limit_bytes=60 * 1024 * 1024
        ),
        name="encoder_layer",
    )(
        tokens, cotangent, w_query, w_key, w_value, w_out, w_inner, w_outer,
        doc_vectors, doc_ids, b_query, b_value, b_out, gain_one, shift_one, b_inner, b_outer,
        gain_two, shift_two,
    )

    inner = n_batch // GROUP
    if inner > 1:
        groups = [[g * inner + i for i in range(inner)] for g in range(GROUP)]
        grads = lax.psum_scatter(
            grads, "batch", scatter_dimension=1, axis_index_groups=groups, tiled=True
        )
        small = lax.psum(small, "batch", axis_index_groups=groups)
        part = lax.axis_index("batch") % inner
        pieces = []
        for row in range(SMALL_ROWS):
            wide = {ROW_BQ: local, ROW_BV: local, ROW_BIN: hidden}.get(row, width)
            size = wide // n_batch
            piece = lax.dynamic_slice(small[row], (part * size,), (size,))
            pieces.append(jnp.pad(piece, (0, LANES - size)))
        small = jnp.stack(pieces)

    out_rows = width // n_batch
    vector = shape((out_rows,), F32)
    vector_local = shape((local // n_batch,), F32)
    square = shape((out_rows, local), F32)
    (
        mixed, tokens_grad, doc_grad, wq_grad, bq_grad, wk_grad, wv_grad, bv_grad, wo_grad, bo_grad, g1_grad, s1_grad,
        wi_grad, bi_grad, w2_grad, b2_grad, g2_grad, s2_grad,
    ) = pl.pallas_call(
        functools.partial(finish_kernel, local),
        out_shape=(
            shape((rows, width), BF16), shape((rows, width), BF16),
            shape((docs_dev, width), F32), square, vector_local, square, square, vector_local,
            square, vector, vector, vector,
            shape((out_rows, hidden), F32), shape((hidden // n_batch,), F32),
            shape((out_rows, hidden), F32), vector, vector, vector,
        ),
        in_specs=[hbm, hbm, hbm, vmem, vmem],
        out_specs=(
            hbm, hbm, vmem, hbm, vmem, hbm, hbm, vmem, hbm, vmem, vmem, vmem, hbm, vmem, hbm,
            vmem, vmem, vmem,
        ),
        scratch_shapes=[
            V((2, rows, width), BF16), V((3, out_rows, hidden), F32), dma((7,)), dma((10,)),
        ],
        name="gradient_outputs",
    )(mixed, tokens_grad, grads, small, docs)
    return (
        mixed, tokens_grad, doc_grad, wq_grad, bq_grad, wk_grad, wv_grad, bv_grad, wo_grad.T,
        bo_grad, g1_grad, s1_grad, wi_grad, bi_grad, w2_grad.T, b2_grad, g2_grad, s2_grad,
    )


def solution(mesh):
    in_specs = (
        P("batch", None), P("batch", None), P("batch"), P(None, "tensor"), P("tensor"),
        P(None, "tensor"), P(None, "tensor"), P("tensor"), P("tensor", None), P(), P(), P(),
        P(None, "tensor"), P("tensor"), P("tensor", None), P(), P(), P(), P("batch", None),
    )
    out_specs = (
        P("batch", None), P("batch", None), P("batch", None), P("batch", "tensor"),
        P(("tensor", "batch")), P("batch", "tensor"), P("batch", "tensor"),
        P(("tensor", "batch")), P("tensor", "batch"), P("batch"), P("batch"), P("batch"),
        P("batch", "tensor"), P(("tensor", "batch")), P("tensor", "batch"), P("batch"),
        P("batch"), P("batch"),
    )
    return jax.shard_map(
        functools.partial(body, mesh.shape["batch"]),
        mesh=mesh, in_specs=in_specs, out_specs=out_specs, check_vma=False,
    )
```

```python
import functools
import math

import jax
import jax.numpy as jnp
from jax import lax
from jax.experimental import pallas as pl
from jax.experimental.pallas import tpu as pltpu
from jax.sharding import PartitionSpec as P

HEAD_DIM = 64
QLEN = 32
LANES = 128
GROUP = 16
EPSILON = 1e-12
F32 = jnp.float32
BF16 = jnp.bfloat16
MESH = pl.DeviceIdType.MESH

ROW_BQ, ROW_BV, ROW_BOUT, ROW_G1, ROW_S1, ROW_BIN, ROW_BOUTER, ROW_G2, ROW_S2 = range(9)
SMALL_ROWS = 16


def product(left, right, left_dim=1, right_dim=0):
    return lax.dot_general(
        left, right, (((left_dim,), (right_dim,)), ((), ())), preferred_element_type=F32
    )


def fold_rows(block):
    return jnp.sum(block.reshape(block.shape[0] // 8, 8, block.shape[1]), axis=0)


def row_mean(block):
    return jnp.mean(block, axis=1, keepdims=True)


def layer_kernel(
    sizes,
    tokens_hbm, cot_hbm, wq_hbm, wk_hbm, wv_hbm, wo_hbm, wi_hbm, w2_hbm,
    docs_ref, ids_ref, bq_ref, bv_ref, bo_ref, g1_ref, s1_ref, bi_ref, b2_ref, g2_ref, s2_ref,
    mixed_out, tgrad_out, grads_out, small_out, docs_out,
    tok, cot, w_qkv, wo_all, wi, w2,
    x_low, qkv_s, p_s, att_all, n1_s, r1_s, h1_low, g_s, sl_s, dz_s, df_s, du_s,
    da_s, dqkv_s, acc, accb, accq, accx,
    y_send, y_recv, ff0, ff1, ff2, ff3, ff4, at0, at1, at2, at3, at4, ss0, ss1, ss2, ss3, ss4,
    doc_stage, doc_table, doc_part, doc_in, sum_send, sum_recv,
    y_ssem, y_rsem, a_ssem, a_rsem, w_ssem, w_rsem, r_ssem, r_rsem, d_ssem, d_rsem,
    s_ssem, s_rsem, load_sem,
):
    n_batch, pairs, seq = sizes
    rows, width = tok.shape
    local = wq_hbm.shape[1]
    hidden = wi.shape[1]
    chunk = width // GROUP
    docs_dev = docs_ref.shape[0]
    doc_cols = width // LANES
    inner = n_batch // GROUP

    b = lax.axis_index("batch")
    t = lax.axis_index("tensor")
    place = b // inner
    rest = b % inner
    core = place % 2
    xpos = (place // 2) % 2
    zlow = (place // 4) % 2
    zhigh = place // 8

    def at_place(other):
        return (other * inner + rest, t)

    y_peer = (b, 1 - t)
    core_peer = at_place(place + 1 - 2 * core)
    x_peer = at_place(place + 2 - 4 * xpos)
    zlow_peer = at_place(place + 4 - 8 * zlow)
    zhigh_peer = at_place(place + 8 - 16 * zhigh)

    def batch_peer(step):
        return ((b + step) % n_batch, t)

    barrier = pltpu.get_barrier_semaphore()

    def greet(step, carry):
        pl.semaphore_signal(barrier, inc=1, device_id=batch_peer(step), device_id_type=MESH)
        return carry

    lax.fori_loop(1, n_batch, greet, 0)
    pl.semaphore_signal(barrier, inc=1, device_id=y_peer, device_id_type=MESH)

    wo_mine = pl.ds(pl.multiple_of(t * local, LANES), local)
    att_mine = wo_mine
    loads = []
    for i, (src, dst) in enumerate(
        (
            (tokens_hbm, tok), (wq_hbm, w_qkv.at[:, 0:local]),
            (wk_hbm, w_qkv.at[:, local : 2 * local]), (wv_hbm, w_qkv.at[:, 2 * local :]),
            (wo_hbm, wo_all.at[wo_mine]), (wi_hbm, wi), (w2_hbm, w2), (cot_hbm, cot),
        )
    ):
        copy = pltpu.make_async_copy(src, dst, load_sem.at[i])
        copy.start()
        loads.append(copy)
    (tok_load, wq_load, wk_load, wv_load, wo_load, wi_load, w2_load, cot_load) = loads

    doc_rows = docs_ref[...].astype(F32)
    pieces = []
    for n in range(docs_dev):
        for j in range(8):
            if j < doc_cols:
                pieces.append(doc_rows[n : n + 1, j * LANES : (j + 1) * LANES])
            else:
                pieces.append(jnp.zeros((1, LANES), F32))
    stage = jnp.concatenate(pieces, axis=0).astype(BF16)
    doc_stage[...] = stage
    doc_table[b] = stage

    b_qkv = jnp.concatenate(
        [
            bq_ref[...].astype(F32).reshape(1, local),
            jnp.zeros((1, local), F32),
            bv_ref[...].astype(F32).reshape(1, local),
        ],
        axis=1,
    )
    b_out = bo_ref[...].astype(F32).reshape(1, width)
    gain1 = g1_ref[...].astype(F32).reshape(1, width)
    shift1 = s1_ref[...].astype(F32).reshape(1, width)
    b_inner = bi_ref[...].astype(F32).reshape(1, hidden)
    b_outer = b2_ref[...].astype(F32).reshape(1, width)
    gain2 = g2_ref[...].astype(F32).reshape(1, width)
    shift2 = s2_ref[...].astype(F32).reshape(1, width)

    pl.semaphore_wait(barrier, n_batch)

    share = local // 4

    def share_rows(tensor, first, count):
        start = tensor * local + first * share
        return pl.ds(pl.multiple_of(start, 16), count * share)

    quarter = 2 * core + xpos
    out_weight_copies = [
        pltpu.make_async_remote_copy(
            src_ref=source,
            dst_ref=wo_all.at[target],
            send_sem=w_ssem.at[i],
            recv_sem=w_rsem.at[i],
            device_id=peer,
            device_id_type=MESH,
        )
        for i, (source, target, peer) in enumerate(
            (
                (
                    wo_hbm.at[pl.ds(pl.multiple_of(quarter * share, 16), share)],
                    share_rows(t, quarter, 1),
                    y_peer,
                ),
                (
                    wo_all.at[share_rows(1 - t, quarter, 1)],
                    share_rows(1 - t, quarter, 1),
                    x_peer,
                ),
                (
                    wo_all.at[share_rows(1 - t, 2 * core, 2)],
                    share_rows(1 - t, 2 * core, 2),
                    core_peer,
                ),
            )
        )
    ]
    out_weight_copies[0].start()

    def doc_copy(step):
        return pltpu.make_async_remote_copy(
            src_ref=doc_stage,
            dst_ref=doc_table.at[b],
            send_sem=d_ssem.at[0, step],
            recv_sem=d_rsem.at[0, b],
            device_id=batch_peer(step),
            device_id_type=MESH,
        )

    def doc_arrival(step):
        other = (b + step) % n_batch
        return pltpu.make_async_remote_copy(
            src_ref=doc_stage,
            dst_ref=doc_table.at[other],
            send_sem=d_ssem.at[0, step],
            recv_sem=d_rsem.at[0, other],
            device_id=batch_peer(step),
            device_id_type=MESH,
        )

    def doc_start(step, carry):
        doc_copy(step).start()
        return carry

    def doc_wait(step, carry):
        doc_arrival(step).wait_recv()
        return carry

    def doc_sent(step, carry):
        doc_copy(step).wait_send()
        return carry

    lax.fori_loop(1, n_batch, doc_start, 0)

    tok_load.wait()
    lax.fori_loop(1, n_batch, doc_wait, 0)

    ids = [jnp.full((8, LANES), ids_ref[p], jnp.int32) for p in range(pairs)]

    def pick(d, found):
        block = doc_table[d].astype(F32)
        result = []
        for p in range(pairs):
            value = found[p]
            for n in range(docs_dev):
                value = value + jnp.where(
                    ids[p] == d * docs_dev + n, block[8 * n : 8 * n + 8, :], 0.0
                )
            result.append(value)
        return tuple(result)

    found = lax.fori_loop(
        0, n_batch, pick, tuple(jnp.zeros((8, LANES), F32) for _ in range(pairs))
    )
    doc_row = [
        jnp.concatenate([found[p][j : j + 1, :] for j in range(doc_cols)], axis=1)
        for p in range(pairs)
    ]

    def pair_rows(p):
        return pl.ds(p * seq, seq)

    def inputs_of(p):
        where_row = lax.broadcasted_iota(jnp.int32, (seq, 1), 0)
        return tok[pair_rows(p), :].astype(F32) + jnp.where(where_row >= QLEN, doc_row[p], 0.0)

    half = width // 2

    def half_cols(part):
        return pl.ds(part * half, half)

    def y_copy(kind, p, part):
        return pltpu.make_async_remote_copy(
            src_ref=y_send.at[kind, p, :, half_cols(part)],
            dst_ref=y_recv.at[kind, p, :, half_cols(part)],
            send_sem=y_ssem.at[kind, p, part],
            recv_sem=y_rsem.at[kind, p, part],
            device_id=y_peer,
            device_id_type=MESH,
        )

    def y_wait(kind, p):
        for part in range(2):
            y_copy(kind, p, part).wait_recv()

    def y_sum(kind, p):
        return y_send[kind, p].astype(F32) + y_recv[kind, p].astype(F32)

    F_SUM, DH_SUM, DX_SUM = range(3)

    def att_cols(tensor, j):
        return pl.ds(pl.multiple_of(tensor * local + j * LANES, LANES), LANES)

    def att_copy(p, j):
        place_of = att_all.at[pair_rows(p), att_cols(t, j)]
        return pltpu.make_async_remote_copy(
            src_ref=place_of,
            dst_ref=place_of,
            send_sem=a_ssem.at[p, j],
            recv_sem=a_rsem.at[p, j],
            device_id=y_peer,
            device_id_type=MESH,
        )

    first_lanes = lax.broadcasted_iota(jnp.int32, (1, LANES), 1) < HEAD_DIM

    def head_lanes(values, h):
        keep = first_lanes if h == 0 else jnp.logical_not(first_lanes)
        return jnp.where(keep, values, jnp.zeros_like(values))

    def both_heads(values):
        return jnp.concatenate([head_lanes(values, 0), head_lanes(values, 1)], axis=0)

    def add_acc(which, p, value):
        if p == 0:
            acc[which] = value
        else:
            acc[which] = acc[which] + value

    A_G2, A_S2, A_BOUTER, A_G1, A_S1, A_BOUT = range(6)

    def project(p):
        mine = pair_rows(p)
        x_low[mine, :] = inputs_of(p).astype(BF16)
        qkv_s[mine, :] = (product(x_low[mine, :], w_qkv[...]) + b_qkv).astype(BF16)

    def qkv(kind, j):
        return pl.ds(kind * local + j * LANES, LANES)

    def attention(p):
        mine = pair_rows(p)
        for j in range(local // LANES):
            kk, vv = qkv_s[mine, qkv(1, j)], qkv_s[mine, qkv(2, j)]
            qq = (qkv_s[mine, qkv(0, j)].astype(F32) * 0.125).astype(BF16)
            qkv_s[mine, qkv(0, j)] = qq
            low = []
            for h in range(2):
                scores = product(head_lanes(qq, h), kk, 1, 1)
                expo = jnp.exp(scores - jnp.max(scores, axis=1, keepdims=True))
                probs = expo * (1.0 / jnp.sum(expo, axis=1, keepdims=True))
                p_s[p * (local // HEAD_DIM) + 2 * j + h] = probs
                low.append(probs.astype(BF16))
            both = product(low[0], head_lanes(vv, 0)) + product(low[1], head_lanes(vv, 1))
            att_all[mine, att_cols(t, j)] = both.astype(BF16)
            att_copy(p, j).start()

    def attention_out(p):
        for j in range(local // LANES):
            att_copy(p, j).wait_recv()
        mine = pair_rows(p)
        summed = inputs_of(p) + (product(att_all[mine, :], wo_all[...]) + b_out)
        centered = summed - row_mean(summed)
        inverse = lax.rsqrt(row_mean(centered * centered) + EPSILON)
        normed = centered * inverse
        n1_s[mine, :] = normed
        r1_s[mine, :] = inverse
        h1_low[mine, :] = (normed * gain1 + shift1).astype(BF16)

    FF_TILE = 512

    def feed_forward(p):
        mine = pair_rows(p)
        u = product(h1_low[mine, :], wi[...]) + b_inner
        cdf = 0.5 * (1.0 + lax.erf(u * (1.0 / math.sqrt(2.0))))
        density = jnp.exp(-0.5 * u * u) * (1.0 / math.sqrt(2.0 * math.pi))
        g_s[mine, :] = (u * cdf).astype(BF16)
        sl_s[mine, :] = cdf + u * density
        for part in range(2):
            cols = half_cols(part)
            y_send[F_SUM, p, :, cols] = product(g_s[mine, :], w2[:, cols]).astype(BF16)
            y_copy(F_SUM, p, part).start()

    def norm_two(p):
        mine = pair_rows(p)
        h1 = n1_s[mine, :] * gain1 + shift1
        summed = h1 + (y_sum(F_SUM, p) + b_outer)
        centered = summed - row_mean(summed)
        inverse = lax.rsqrt(row_mean(centered * centered) + EPSILON)
        normed = centered * inverse
        mixed_out[mine, :] = (normed * gain2 + shift2).astype(BF16)
        dy = cot[mine, :].astype(F32)
        scaled = dy * gain2
        dz = inverse * (scaled - row_mean(scaled) - normed * row_mean(scaled * normed))
        dz_s[mine, :] = dz
        df_s[mine, :] = dz.astype(BF16)
        add_acc(A_G2, p, fold_rows(dy * normed))
        add_acc(A_S2, p, fold_rows(dy))
        add_acc(A_BOUTER, p, fold_rows(dz))

    def feed_forward_back(p):
        mine = pair_rows(p)
        du = (product(df_s[mine, :], w2[...], 1, 1) * sl_s[mine, :]).astype(BF16)
        du_s[mine, :] = du
        total = fold_rows(du.astype(F32))
        if p == 0:
            accb[...] = total
        else:
            accb[...] = accb[...] + total
        for part in range(2):
            cols = half_cols(part)
            y_send[DH_SUM, p, :, cols] = product(du_s[mine, :], wi[cols, :], 1, 1).astype(BF16)
            y_copy(DH_SUM, p, part).start()

    def norm_one_back(p):
        mine = pair_rows(p)
        dh = dz_s[mine, :] + y_sum(DH_SUM, p)
        normed = n1_s[mine, :]
        scaled = dh * gain1
        dz = r1_s[mine, :] * (scaled - row_mean(scaled) - normed * row_mean(scaled * normed))
        dz_s[mine, :] = dz
        df_s[mine, :] = dz.astype(BF16)
        doc_part_rows = fold_rows(dz[QLEN:, :])
        accx[p] = doc_part_rows
        add_acc(A_G1, p, fold_rows(dh * normed))
        add_acc(A_S1, p, fold_rows(dh))
        add_acc(A_BOUT, p, doc_part_rows + fold_rows(dz[:QLEN, :]))

    def attention_back(p):
        mine = pair_rows(p)
        da_s[mine, :] = product(df_s[mine, :], wo_all[wo_mine, :], 1, 1).astype(BF16)
        for j in range(local // LANES):
            qq, kk, vv = (qkv_s[mine, qkv(kind, j)] for kind in range(3))
            dd = da_s[mine, pl.ds(j * LANES, LANES)]
            low, ds = [], []
            for h in range(2):
                probs = p_s[p * (local // HEAD_DIM) + 2 * j + h]
                low.append(probs.astype(BF16))
                dp = product(head_lanes(dd, h), vv, 1, 1)
                slope = probs * (dp - jnp.sum(probs * dp, axis=1, keepdims=True))
                ds.append(slope.astype(BF16))
            dv = product(jnp.concatenate(low, axis=0), both_heads(dd), 0, 0)
            dk = product(jnp.concatenate(ds, axis=0), both_heads(qq), 0, 0)
            dq = product(ds[0], head_lanes(kk, 0)) + product(ds[1], head_lanes(kk, 1))
            dqkv_s[mine, qkv(0, j)] = (dq * 0.125).astype(BF16)
            dqkv_s[mine, qkv(1, j)] = dk.astype(BF16)
            dqkv_s[mine, qkv(2, j)] = dv.astype(BF16)
        for i, kind in enumerate((0, 2)):
            total = fold_rows(dqkv_s[mine, pl.ds(kind * local, local)].astype(F32))
            if p == 0:
                accq[i] = total
            else:
                accq[i] = accq[i] + total

    def inputs_back(p):
        mine = pair_rows(p)
        part = product(dqkv_s[mine, :], w_qkv[...], 1, 1)
        y_send[DX_SUM, p] = part.astype(BF16)
        accx[p] = jnp.where(t == 0, accx[p], 0.0) + fold_rows(part[QLEN:, :])

    def inputs_send(p):
        for part in range(2):
            y_copy(DX_SUM, p, part).start()

    N_FF = 6
    N_PIECES = 11
    X_Z, Z_X_Z, Z_Z_X = (0, 1, 2, 3), (0, 2, 1, 3), (0, 2, 3, 1)
    HALVING = (Z_Z_X, X_Z, Z_Z_X, X_Z, X_Z, X_Z, X_Z, X_Z, X_Z, Z_X_Z, X_Z)

    def piece_refs(m):
        if m < N_FF:
            return [ref.at[m] for ref in (ff0, ff1, ff2, ff3, ff4)]
        if m < N_PIECES - 1:
            return [ref.at[m - N_FF] for ref in (at0, at1, at2, at3, at4)]
        return [ss0, ss1, ss2, ss3, ss4]

    def chunk_index(m, r):
        bits = (r % 2, (r // 2) % 2, (r // 4) % 2, r // 8)
        return tuple(bits[k] for k in HALVING[m])

    def my_index(m):
        return tuple((core, xpos, zlow, zhigh)[k] for k in HALVING[m])

    def piece_copy(m, phase):
        refs = piece_refs(m)
        index = my_index(m)
        peers = (core_peer, x_peer, zlow_peer, zhigh_peer)
        return pltpu.make_async_remote_copy(
            src_ref=refs[0].at[(*index[:phase], 1 - index[phase])],
            dst_ref=refs[phase + 1],
            send_sem=r_ssem.at[m, phase],
            recv_sem=r_rsem.at[m, phase],
            device_id=peers[HALVING[m][phase]],
            device_id_type=MESH,
        )

    def add_piece(mine, index, other, lead):
        if lead == 0:
            value = mine[index].astype(F32) + other[...].astype(F32)
            mine[index] = value.astype(mine.dtype)
            return
        for k in range(2):
            add_piece(mine, (*index, k), other.at[k], lead - 1)

    def advance(m, phase):
        refs = piece_refs(m)
        index = my_index(m)
        piece_copy(m, phase - 1).wait_recv()
        mine, other = refs[0], refs[phase]
        away, stay = 1 - index[phase], index[phase]
        add_piece(mine, (*index[:phase], away), other.at[away], 3 - phase)
        piece_copy(m, phase).start()
        add_piece(mine, (*index[:phase], stay), other.at[stay], 3 - phase)

    def complete(m):
        refs = piece_refs(m)
        index = my_index(m)
        piece_copy(m, 3).wait_recv()
        total = refs[0][index].astype(F32) + refs[4][...].astype(F32)
        if m < N_FF:
            grads_out[m // 3, :, (m % 3) * FF_TILE : (m % 3 + 1) * FF_TILE] = total
        elif m < N_PIECES - 1:
            n = m - N_FF
            grads_out[2, :, n * local : (n + 1) * local] = total
        else:
            small_out[...] = total

    def weight_grad(m, left, right):
        refs = piece_refs(m)
        grad = product(left, right, 0, 0)
        for r in range(GROUP):
            refs[0][chunk_index(m, r)] = grad[r * chunk : (r + 1) * chunk, :].astype(BF16)
        piece_copy(m, 0).start()

    def outer_grad(n):
        weight_grad(n, df_s[...], g_s[:, n * FF_TILE : (n + 1) * FF_TILE])

    def inner_grad(n):
        weight_grad(3 + n, h1_low[...], du_s[:, n * FF_TILE : (n + 1) * FF_TILE])

    def place_vector(row, eight):
        vector = jnp.sum(eight, axis=0, keepdims=True)
        piece = vector.shape[1] // GROUP
        for r in range(GROUP):
            ss0[(*chunk_index(SMALL, r), slice(row, row + 1), slice(0, piece))] = vector[
                :, r * piece : (r + 1) * piece
            ]

    OUT, QUERY, KEY, VALUE, SMALL = range(N_FF, N_PIECES)

    def qkv_grad(m):
        kind = m - QUERY
        weight_grad(m, x_low[...], dqkv_s[:, kind * local : (kind + 1) * local])

    zero_row = jnp.zeros((1, LANES), F32)
    sum_copy = pltpu.make_async_remote_copy(
        src_ref=sum_send,
        dst_ref=sum_recv,
        send_sem=s_ssem.at[0],
        recv_sem=s_rsem.at[0],
        device_id=y_peer,
        device_id_type=MESH,
    )

    def send_document_sums():
        for p in range(pairs):
            row = jnp.sum(accx[p], axis=0, keepdims=True)
            sum_send[p] = jnp.concatenate(
                [row[:, j * LANES : (j + 1) * LANES] for j in range(doc_cols)]
                + [zero_row] * (8 - doc_cols),
                axis=0,
            )
        sum_copy.start()

    def part_copy(step):
        other = (b + step) % n_batch
        return pltpu.make_async_remote_copy(
            src_ref=doc_part.at[other],
            dst_ref=doc_in.at[b],
            send_sem=d_ssem.at[1, step],
            recv_sem=d_rsem.at[1, b],
            device_id=(other, t),
            device_id_type=MESH,
        )

    def part_arrival(step):
        other = (b + step) % n_batch
        return pltpu.make_async_remote_copy(
            src_ref=doc_part.at[other],
            dst_ref=doc_in.at[other],
            send_sem=d_ssem.at[1, step],
            recv_sem=d_rsem.at[1, other],
            device_id=(other, t),
            device_id_type=MESH,
        )

    def part_start(step, carry):
        part_copy(step).start()
        return carry

    def part_wait(step, carry):
        part_arrival(step).wait_recv()
        return carry

    def part_sent(step, carry):
        part_copy(step).wait_send()
        return carry

    def send_document_parts():
        sum_copy.wait_recv()
        sum_blocks = [sum_send[p] + sum_recv[p] for p in range(pairs)]

        def fill(d, carry):
            for n in range(docs_dev):
                value = jnp.zeros((8, LANES), F32)
                for p in range(pairs):
                    value = value + jnp.where(ids[p] == d * docs_dev + n, sum_blocks[p], 0.0)
                doc_part[d, 8 * n : 8 * n + 8, :] = value
            return carry

        lax.fori_loop(0, n_batch, fill, 0)
        lax.fori_loop(1, n_batch, part_start, 0)
        doc_in[b] = doc_part[b]

    def add_document_parts():
        lax.fori_loop(1, n_batch, part_wait, 0)

        def add_part(d, total):
            return total + doc_in[d]

        docs_out[...] = lax.fori_loop(0, n_batch, add_part, jnp.zeros(docs_out.shape, F32))

    def input_grad(p):
        y_wait(DX_SUM, p)
        tgrad_out[pair_rows(p), :] = (dz_s[pair_rows(p), :] + y_sum(DX_SUM, p)).astype(BF16)

    wq_load.wait()
    wk_load.wait()
    wv_load.wait()
    project(0)
    out_weight_copies[0].wait_recv()
    out_weight_copies[1].start()
    attention(0)
    project(1)
    attention(1)
    out_weight_copies[1].wait_recv()
    out_weight_copies[2].start()
    wo_load.wait()
    out_weight_copies[2].wait_recv()
    wi_load.wait()
    w2_load.wait()
    attention_out(0)
    feed_forward(0)
    attention_out(1)
    feed_forward(1)
    cot_load.wait()
    y_wait(F_SUM, 0)
    norm_two(0)
    feed_forward_back(0)
    y_wait(F_SUM, 1)
    norm_two(1)
    outer_grad(2)
    outer_grad(1)
    outer_grad(0)
    advance(2, 1)
    advance(1, 1)
    feed_forward_back(1)
    inner_grad(1)
    advance(0, 1)
    inner_grad(0)
    advance(4, 1)
    advance(3, 1)
    advance(2, 2)
    inner_grad(2)
    advance(1, 2)
    y_wait(DH_SUM, 0)
    norm_one_back(0)
    attention_back(0)
    inputs_back(0)
    inputs_send(0)
    advance(0, 2)
    ss0[...] = jnp.zeros(ss0.shape, F32)
    place_vector(ROW_G2, acc[A_G2])
    place_vector(ROW_S2, acc[A_S2])
    place_vector(ROW_BOUTER, acc[A_BOUTER])
    place_vector(ROW_BIN, accb[...])
    advance(5, 1)
    advance(4, 2)
    advance(1, 3)
    advance(2, 3)
    y_wait(DH_SUM, 1)
    norm_one_back(1)
    weight_grad(OUT, df_s[...], att_all[:, att_mine])
    advance(3, 2)
    attention_back(1)
    advance(4, 3)
    advance(OUT, 1)
    qkv_grad(KEY)
    advance(5, 2)
    qkv_grad(VALUE)
    qkv_grad(QUERY)
    advance(KEY, 1)
    advance(3, 3)
    complete(2)
    advance(VALUE, 1)
    advance(QUERY, 1)
    place_vector(ROW_G1, acc[A_G1])
    place_vector(ROW_S1, acc[A_S1])
    place_vector(ROW_BOUT, acc[A_BOUT])
    place_vector(ROW_BQ, accq[0])
    place_vector(ROW_BV, accq[1])
    piece_copy(SMALL, 0).start()
    advance(OUT, 2)
    inputs_back(1)
    send_document_sums()
    inputs_send(1)
    advance(5, 3)
    advance(KEY, 2)
    advance(VALUE, 2)
    send_document_parts()
    advance(OUT, 3)
    advance(SMALL, 1)
    advance(0, 3)
    advance(QUERY, 2)
    advance(VALUE, 3)
    complete(1)
    complete(5)
    input_grad(0)
    advance(SMALL, 2)
    advance(KEY, 3)
    complete(3)
    advance(QUERY, 3)
    advance(SMALL, 3)
    input_grad(1)
    complete(KEY)
    add_document_parts()
    complete(4)
    complete(OUT)
    complete(VALUE)
    complete(0)
    complete(QUERY)
    complete(SMALL)
    for copy in out_weight_copies:
        copy.wait_send()
    sum_copy.wait_send()
    for p in range(pairs):
        for j in range(local // LANES):
            att_copy(p, j).wait_send()
        for kind in range(3):
            for part in range(2):
                y_copy(kind, p, part).wait_send()
    for m in range(N_PIECES):
        for phase in range(4):
            piece_copy(m, phase).wait_send()
    lax.fori_loop(1, n_batch, doc_sent, 0)
    lax.fori_loop(1, n_batch, part_sent, 0)


def finish_kernel(
    local, mixed_ref, tgrad_ref, grads_ref, small_ref, docs_ref,
    mixed_out, tgrad_out, doc_out, wq_out, bq_out, wk_out, wv_out, bv_out, wo_out, bo_out,
    g1_out, s1_out, wi_out, bi_out, w2_out, b2_out, g2_out, s2_out,
    out_sem,
):
    moves = [(mixed_ref, mixed_out), (tgrad_ref, tgrad_out), (grads_ref.at[0], w2_out)]
    moves.append((grads_ref.at[1], wi_out))
    for n, target in enumerate((wo_out, wq_out, wk_out, wv_out)):
        moves.append((grads_ref.at[2, :, pl.ds(n * local, local)], target))
    copies = [
        pltpu.make_async_copy(source, target, out_sem.at[i])
        for i, (source, target) in enumerate(moves)
    ]
    for copy in copies:
        copy.start()
    docs_dev, width = doc_out.shape
    for n in range(docs_dev):
        for j in range(width // LANES):
            doc_out[n : n + 1, j * LANES : (j + 1) * LANES] = docs_ref[8 * n + j : 8 * n + j + 1, :]
    for row, out in (
        (ROW_BQ, bq_out), (ROW_BV, bv_out), (ROW_BOUT, bo_out), (ROW_G1, g1_out),
        (ROW_S1, s1_out), (ROW_BIN, bi_out), (ROW_BOUTER, b2_out), (ROW_G2, g2_out),
        (ROW_S2, s2_out),
    ):
        out[...] = small_ref[row, 0 : out.shape[0]]
    for copy in copies:
        copy.wait()


def body(
    n_batch,
    tokens, doc_vectors, doc_ids, w_query, b_query, w_key, w_value, b_value, w_out, b_out,
    gain_one, shift_one, w_inner, b_inner, w_outer, b_outer, gain_two, shift_two, cotangent,
):
    rows, width = tokens.shape
    pairs = doc_ids.shape[0]
    seq = rows // pairs
    local = w_query.shape[1]
    heads = local // HEAD_DIM
    hidden = w_inner.shape[1]
    docs_dev = doc_vectors.shape[0]
    chunk = width // GROUP
    part = hidden // 3
    hbm = pl.BlockSpec(memory_space=pl.ANY)
    vmem = pl.BlockSpec(memory_space=pltpu.VMEM)
    smem = pl.BlockSpec(memory_space=pltpu.SMEM)
    V = pltpu.VMEM
    dma = pltpu.SemaphoreType.DMA
    scratch = [
        V((rows, width), BF16), V((rows, width), BF16),
        V((width, 3 * local), BF16), V((width, width), BF16), V((width, hidden), BF16), V((hidden, width), BF16),
        V((rows, width), BF16),
        V((rows, 3 * local), BF16),
        V((pairs * heads, seq, seq), F32),
        V((rows, width), BF16),
        V((rows, width), F32), V((rows, 1), F32), V((rows, width), BF16),
        V((rows, hidden), BF16), V((rows, hidden), F32),
        V((rows, width), F32), V((rows, width), BF16), V((rows, hidden), BF16),
        V((rows, local), BF16), V((rows, 3 * local), BF16),
        V((6, 8, width), F32), V((8, hidden), F32), V((2, 8, local), F32),
        V((pairs, 8, width), F32),
        V((3, pairs, seq, width), BF16), V((3, pairs, seq, width), BF16),
        *[V((6, *(2,) * n, chunk, part), BF16) for n in (4, 3, 2, 1, 0)],
        *[V((4, *(2,) * n, chunk, local), BF16) for n in (4, 3, 2, 1, 0)],
        *[V((*(2,) * n, SMALL_ROWS, LANES), F32) for n in (4, 3, 2, 1, 0)],
        V((8 * docs_dev, LANES), BF16), V((n_batch, 8 * docs_dev, LANES), BF16),
        V((n_batch, 8 * docs_dev, LANES), F32), V((n_batch, 8 * docs_dev, LANES), F32),
        V((pairs, 8, LANES), F32), V((pairs, 8, LANES), F32),
        dma((3, pairs, 2)), dma((3, pairs, 2)), dma((pairs, local // LANES)),
        dma((pairs, local // LANES)), dma((3,)), dma((3,)), dma((11, 4)), dma((11, 4)),
        dma((2, n_batch)), dma((2, n_batch)), dma((1,)), dma((1,)), dma((8,)),
    ]
    shape = jax.ShapeDtypeStruct
    mixed, tokens_grad, grads, small, docs = pl.pallas_call(
        functools.partial(layer_kernel, (n_batch, pairs, seq)),
        out_shape=(
            V((rows, width), BF16),
            V((rows, width), BF16),
            V((3, chunk, hidden), F32),
            V((SMALL_ROWS, LANES), F32),
            V((8 * docs_dev, LANES), F32),
        ),
        in_specs=[hbm] * 8 + [vmem, smem] + [vmem] * 9,
        out_specs=(vmem,) * 5,
        scratch_shapes=scratch,
        compiler_params=pltpu.CompilerParams(
            collective_id=0, has_side_effects=True, vmem_limit_bytes=60 * 1024 * 1024
        ),
        name="encoder_layer",
    )(
        tokens, cotangent, w_query, w_key, w_value, w_out, w_inner, w_outer,
        doc_vectors, doc_ids, b_query, b_value, b_out, gain_one, shift_one, b_inner, b_outer,
        gain_two, shift_two,
    )

    inner = n_batch // GROUP
    if inner > 1:
        groups = [[g * inner + i for i in range(inner)] for g in range(GROUP)]
        grads = lax.psum_scatter(
            grads, "batch", scatter_dimension=1, axis_index_groups=groups, tiled=True
        )
        small = lax.psum(small, "batch", axis_index_groups=groups)
        part = lax.axis_index("batch") % inner
        pieces = []
        for row in range(SMALL_ROWS):
            wide = {ROW_BQ: local, ROW_BV: local, ROW_BIN: hidden}.get(row, width)
            size = wide // n_batch
            piece = lax.dynamic_slice(small[row], (part * size,), (size,))
            pieces.append(jnp.pad(piece, (0, LANES - size)))
        small = jnp.stack(pieces)

    if inner == 1:
        mixed, tokens_grad, grads, small, docs = (
            pltpu.with_memory_space_constraint(item, pltpu.VMEM)
            for item in (mixed, tokens_grad, grads, small, docs)
        )
    out_rows = width // n_batch
    vector = shape((out_rows,), F32)
    vector_local = shape((local // n_batch,), F32)
    square = shape((out_rows, local), F32)
    (
        mixed, tokens_grad, doc_grad, wq_grad, bq_grad, wk_grad, wv_grad, bv_grad, wo_grad, bo_grad, g1_grad, s1_grad,
        wi_grad, bi_grad, w2_grad, b2_grad, g2_grad, s2_grad,
    ) = pl.pallas_call(
        functools.partial(finish_kernel, local),
        out_shape=(
            shape((rows, width), BF16), shape((rows, width), BF16),
            shape((docs_dev, width), F32), square, vector_local, square, square, vector_local,
            square, vector, vector, vector,
            shape((out_rows, hidden), F32), shape((hidden // n_batch,), F32),
            shape((out_rows, hidden), F32), vector, vector, vector,
        ),
        in_specs=[vmem] * 5,
        out_specs=(
            hbm, hbm, vmem, hbm, vmem, hbm, hbm, vmem, hbm, vmem, vmem, vmem, hbm, vmem, hbm,
            vmem, vmem, vmem,
        ),
        scratch_shapes=[dma((8,))],
        name="gradient_outputs",
    )(mixed, tokens_grad, grads, small, docs)
    return (
        mixed, tokens_grad, doc_grad, wq_grad, bq_grad, wk_grad, wv_grad, bv_grad, wo_grad.T,
        bo_grad, g1_grad, s1_grad, wi_grad, bi_grad, w2_grad.T, b2_grad, g2_grad, s2_grad,
    )


def solution(mesh):
    in_specs = (
        P("batch", None), P("batch", None), P("batch"), P(None, "tensor"), P("tensor"),
        P(None, "tensor"), P(None, "tensor"), P("tensor"), P("tensor", None), P(), P(), P(),
        P(None, "tensor"), P("tensor"), P("tensor", None), P(), P(), P(), P("batch", None),
    )
    out_specs = (
        P("batch", None), P("batch", None), P("batch", None), P("batch", "tensor"),
        P(("tensor", "batch")), P("batch", "tensor"), P("batch", "tensor"),
        P(("tensor", "batch")), P("tensor", "batch"), P("batch"), P("batch"), P("batch"),
        P("batch", "tensor"), P(("tensor", "batch")), P("tensor", "batch"), P("batch"),
        P("batch"), P("batch"),
    )
    return jax.shard_map(
        functools.partial(body, mesh.shape["batch"]),
        mesh=mesh, in_specs=in_specs, out_specs=out_specs, check_vma=False,
    )
```

```python
import functools
import math

import jax
import jax.numpy as jnp
from jax import lax
from jax.experimental import pallas as pl
from jax.experimental.pallas import tpu as pltpu
from jax.sharding import PartitionSpec as P

HEAD_DIM = 64
QLEN = 32
LANES = 128
GROUP = 16
EPSILON = 1e-12
F32 = jnp.float32
BF16 = jnp.bfloat16
MESH = pl.DeviceIdType.MESH

ROW_BQ, ROW_BV, ROW_BOUT, ROW_G1, ROW_S1, ROW_BIN, ROW_BOUTER, ROW_G2, ROW_S2 = range(9)
SMALL_ROWS = 16


def product(left, right, left_dim=1, right_dim=0):
    return lax.dot_general(
        left, right, (((left_dim,), (right_dim,)), ((), ())), preferred_element_type=F32
    )


def fold_rows(block):
    return jnp.sum(block.reshape(block.shape[0] // 8, 8, block.shape[1]), axis=0)


def row_mean(block):
    return jnp.mean(block, axis=1, keepdims=True)


def layer_kernel(
    sizes,
    tokens_hbm, cot_hbm, wq_hbm, wk_hbm, wv_hbm, wo_hbm, wi_hbm, w2_hbm,
    docs_hbm, ids_hbm, bq_hbm, bv_hbm, bo_hbm, g1_hbm, s1_hbm, bi_hbm, b2_hbm, g2_hbm, s2_hbm,
    mixed_out, tgrad_out, grads_out, small_out, docs_out,
    docs_ref, ids_ref, bq_ref, bv_ref, bo_ref, g1_ref, s1_ref, bi_ref, b2_ref, g2_ref, s2_ref,
    tok, cot, w_qkv, wo_all, wi, w2,
    x_low, qkv_s, p_s, att_all, n1_s, r1_s, h1_low, g_s, sl_s, dz_s, df_s, du_s,
    da_s, dqkv_s, acc, accb, accq, accx,
    y_send, y_recv, ff0, ff1, ff2, ff3, ff4, at0, at1, at2, at3, at4,
    va0, va1, va2, va3, va4, vb0, vb1, vb2, vb3, vb4, ss0, ss1, ss2, ss3, ss4,
    doc_stage, doc_table, doc_part, doc_in, sum_send, sum_recv,
    y_ssem, y_rsem, a_ssem, a_rsem, w_ssem, w_rsem, r_ssem, r_rsem, d_ssem, d_rsem,
    s_ssem, s_rsem, load_sem,
):
    n_batch, pairs, seq = sizes
    rows, width = tok.shape
    local = wq_hbm.shape[1]
    hidden = wi.shape[1]
    chunk = width // GROUP
    docs_dev = docs_ref.shape[0]
    doc_cols = width // LANES
    inner = n_batch // GROUP

    b = lax.axis_index("batch")
    t = lax.axis_index("tensor")
    place = b // inner
    rest = b % inner
    core = place % 2
    xpos = (place // 2) % 2
    zlow = (place // 4) % 2
    zhigh = place // 8

    def at_place(other):
        return (other * inner + rest, t)

    y_peer = (b, 1 - t)
    core_peer = at_place(place + 1 - 2 * core)
    x_peer = at_place(place + 2 - 4 * xpos)
    zlow_peer = at_place(place + 4 - 8 * zlow)
    zhigh_peer = at_place(place + 8 - 16 * zhigh)

    def batch_peer(step):
        return ((b + step) % n_batch, t)

    def doc_steps(step):
        if n_batch <= GROUP:
            for i in range(1, n_batch):
                step(i, 0)
        else:
            lax.fori_loop(1, n_batch, step, 0)

    barrier = pltpu.get_barrier_semaphore()

    def greet(step, carry):
        pl.semaphore_signal(barrier, inc=1, device_id=batch_peer(step), device_id_type=MESH)
        return carry

    doc_steps(greet)
    pl.semaphore_signal(barrier, inc=1, device_id=y_peer, device_id_type=MESH)

    wo_mine = pl.ds(pl.multiple_of(t * local, LANES), local)
    att_mine = wo_mine
    loads = []
    vectors = (
        (bq_hbm, bq_ref), (bv_hbm, bv_ref), (bo_hbm, bo_ref), (g1_hbm, g1_ref), (s1_hbm, s1_ref),
        (bi_hbm, bi_ref), (b2_hbm, b2_ref), (g2_hbm, g2_ref), (s2_hbm, s2_ref),
    )
    head_pairs = local // LANES
    group = 3 * LANES
    qkv_weights = [
        (
            source.at[:, pl.ds(j * LANES, LANES)],
            w_qkv.at[:, pl.ds(j * group + kind * LANES, LANES)],
        )
        for j in range(head_pairs)
        for kind, source in enumerate((wq_hbm, wk_hbm, wv_hbm))
    ]
    for i, (src, dst) in enumerate(
        (
            (docs_hbm, docs_ref), (ids_hbm, ids_ref), *vectors,
            (tokens_hbm, tok), *qkv_weights,
            (wo_hbm, wo_all.at[wo_mine]), (wi_hbm, wi), (w2_hbm, w2), (cot_hbm, cot),
        )
    ):
        copy = pltpu.make_async_copy(src, dst, load_sem.at[i])
        copy.start()
        loads.append(copy)
    docs_load, ids_load = loads[:2]
    tok_load, *qkv_loads = loads[2 + len(vectors) : -4]
    wo_load, wi_load, w2_load, cot_load = loads[-4:]
    docs_load.wait()

    doc_rows = docs_ref[...].astype(F32)
    pieces = []
    for n in range(docs_dev):
        for j in range(8):
            if j < doc_cols:
                pieces.append(doc_rows[n : n + 1, j * LANES : (j + 1) * LANES])
            else:
                pieces.append(jnp.zeros((1, LANES), F32))
    stage = jnp.concatenate(pieces, axis=0).astype(BF16)
    doc_stage[...] = stage
    doc_table[b] = stage

    pl.semaphore_wait(barrier, n_batch)

    share = local // 4

    def share_rows(tensor, first, count):
        start = tensor * local + first * share
        return pl.ds(pl.multiple_of(start, 16), count * share)

    quarter = 2 * core + xpos
    out_weight_copies = [
        pltpu.make_async_remote_copy(
            src_ref=source,
            dst_ref=wo_all.at[target],
            send_sem=w_ssem.at[i],
            recv_sem=w_rsem.at[i],
            device_id=peer,
            device_id_type=MESH,
        )
        for i, (source, target, peer) in enumerate(
            (
                (
                    wo_hbm.at[pl.ds(pl.multiple_of(quarter * share, 16), share)],
                    share_rows(t, quarter, 1),
                    y_peer,
                ),
                (
                    wo_all.at[share_rows(1 - t, quarter, 1)],
                    share_rows(1 - t, quarter, 1),
                    x_peer,
                ),
                (
                    wo_all.at[share_rows(1 - t, 2 * core, 2)],
                    share_rows(1 - t, 2 * core, 2),
                    core_peer,
                ),
            )
        )
    ]
    out_weight_copies[0].start()

    def doc_copy(step):
        return pltpu.make_async_remote_copy(
            src_ref=doc_stage,
            dst_ref=doc_table.at[b],
            send_sem=d_ssem.at[0, step],
            recv_sem=d_rsem.at[0, b],
            device_id=batch_peer(step),
            device_id_type=MESH,
        )

    def doc_arrival(step):
        other = (b + step) % n_batch
        return pltpu.make_async_remote_copy(
            src_ref=doc_stage,
            dst_ref=doc_table.at[other],
            send_sem=d_ssem.at[0, step],
            recv_sem=d_rsem.at[0, other],
            device_id=batch_peer(step),
            device_id_type=MESH,
        )

    def doc_start(step, carry):
        doc_copy(step).start()
        return carry

    def doc_wait(step, carry):
        doc_arrival(step).wait_recv()
        return carry

    def doc_sent(step, carry):
        doc_copy(step).wait_send()
        return carry

    doc_steps(doc_start)

    for copy in loads[2 : 2 + len(vectors)]:
        copy.wait()
    b_query = bq_ref[...].astype(F32).reshape(1, local)
    b_value = bv_ref[...].astype(F32).reshape(1, local)
    b_out = bo_ref[...].astype(F32).reshape(1, width)
    gain1 = g1_ref[...].astype(F32).reshape(1, width)
    shift1 = s1_ref[...].astype(F32).reshape(1, width)
    b_inner = bi_ref[...].astype(F32).reshape(1, hidden)
    b_outer = b2_ref[...].astype(F32).reshape(1, width)
    gain2 = g2_ref[...].astype(F32).reshape(1, width)
    shift2 = s2_ref[...].astype(F32).reshape(1, width)

    tok_load.wait()
    doc_steps(doc_wait)

    ids_load.wait()
    ids = [jnp.full((8, LANES), ids_ref[p], jnp.int32) for p in range(pairs)]

    def pick(d, found):
        block = doc_table[d].astype(F32)
        result = []
        for p in range(pairs):
            value = found[p]
            for n in range(docs_dev):
                value = value + jnp.where(
                    ids[p] == d * docs_dev + n, block[8 * n : 8 * n + 8, :], 0.0
                )
            result.append(value)
        return tuple(result)

    found = lax.fori_loop(
        0, n_batch, pick, tuple(jnp.zeros((8, LANES), F32) for _ in range(pairs))
    )
    doc_row = [
        jnp.concatenate([found[p][j : j + 1, :] for j in range(doc_cols)], axis=1)
        for p in range(pairs)
    ]

    def pair_rows(p):
        return pl.ds(p * seq, seq)

    def inputs_of(p):
        where_row = lax.broadcasted_iota(jnp.int32, (seq, 1), 0)
        return tok[pair_rows(p), :].astype(F32) + jnp.where(where_row >= QLEN, doc_row[p], 0.0)

    half = width // 2

    def half_cols(part):
        return pl.ds(part * half, half)

    def y_copy(kind, p, part):
        return pltpu.make_async_remote_copy(
            src_ref=y_send.at[kind, p, :, half_cols(part)],
            dst_ref=y_recv.at[kind, p, :, half_cols(part)],
            send_sem=y_ssem.at[kind, p, part],
            recv_sem=y_rsem.at[kind, p, part],
            device_id=y_peer,
            device_id_type=MESH,
        )

    def y_wait(kind, p):
        for part in range(2):
            y_copy(kind, p, part).wait_recv()

    def y_sum(kind, p):
        return y_send[kind, p].astype(F32) + y_recv[kind, p].astype(F32)

    F_SUM, DH_SUM, DX_SUM = range(3)

    def att_cols(tensor, j):
        return pl.ds(pl.multiple_of(tensor * local + j * LANES, LANES), LANES)

    def att_copy(p, j):
        place_of = att_all.at[pair_rows(p), att_cols(t, j)]
        return pltpu.make_async_remote_copy(
            src_ref=place_of,
            dst_ref=place_of,
            send_sem=a_ssem.at[p, j],
            recv_sem=a_rsem.at[p, j],
            device_id=y_peer,
            device_id_type=MESH,
        )

    first_lanes = lax.broadcasted_iota(jnp.int32, (1, LANES), 1) < HEAD_DIM

    def head_lanes(values, h):
        keep = first_lanes if h == 0 else jnp.logical_not(first_lanes)
        return jnp.where(keep, values, jnp.zeros_like(values))

    def both_heads(values):
        return jnp.concatenate([head_lanes(values, 0), head_lanes(values, 1)], axis=0)

    def add_acc(which, p, value):
        if p == 0:
            acc[which] = value
        else:
            acc[which] = acc[which] + value

    A_G2, A_S2, A_BOUTER, A_G1, A_S1, A_BOUT = range(6)

    def project(p):
        mine = pair_rows(p)
        x_low[mine, :] = inputs_of(p).astype(BF16)
        qkv_s[mine, :] = (product(x_low[mine, :], w_qkv[...]) + b_qkv).astype(BF16)

    def qkv(kind, j):
        return pl.ds(j * group + kind * LANES, LANES)

    def make_inputs(p):
        x_low[pair_rows(p), :] = inputs_of(p).astype(BF16)

    def attention(p, j):
        mine = pair_rows(p)
        here = pl.ds(j * LANES, LANES)
        if p == 0:
            for copy in qkv_loads[3 * j : 3 * j + 3]:
                copy.wait()
        both = product(x_low[mine, :], w_qkv[:, pl.ds(j * group, group)])
        qq = (both[:, 0:LANES] + b_query[:, j * LANES : (j + 1) * LANES]).astype(BF16)
        qq = (qq.astype(F32) * 0.125).astype(BF16)
        kk = both[:, LANES : 2 * LANES].astype(BF16)
        vv = (both[:, 2 * LANES :] + b_value[:, j * LANES : (j + 1) * LANES]).astype(BF16)
        qkv_s[mine, qkv(0, j)] = qq
        qkv_s[mine, qkv(1, j)] = kk
        qkv_s[mine, qkv(2, j)] = vv
        low = []
        for h in range(2):
            scores = product(head_lanes(qq, h), kk, 1, 1)
            expo = jnp.exp(scores - jnp.max(scores, axis=1, keepdims=True))
            probs = expo * (1.0 / jnp.sum(expo, axis=1, keepdims=True))
            p_s[p * (local // HEAD_DIM) + 2 * j + h] = probs
            low.append(probs.astype(BF16))
        out = product(low[0], head_lanes(vv, 0)) + product(low[1], head_lanes(vv, 1))
        att_all[mine, att_cols(t, j)] = out.astype(BF16)
        att_copy(p, j).start()

    def attention_out(p):
        for j in range(local // LANES):
            att_copy(p, j).wait_recv()
        mine = pair_rows(p)
        summed = inputs_of(p) + (product(att_all[mine, :], wo_all[...]) + b_out)
        centered = summed - row_mean(summed)
        inverse = lax.rsqrt(row_mean(centered * centered) + EPSILON)
        normed = centered * inverse
        n1_s[mine, :] = normed
        r1_s[mine, :] = inverse
        h1_low[mine, :] = (normed * gain1 + shift1).astype(BF16)

    FF_TILE = 512

    def feed_forward(p):
        mine = pair_rows(p)
        u = product(h1_low[mine, :], wi[...]) + b_inner
        cdf = 0.5 * (1.0 + lax.erf(u * (1.0 / math.sqrt(2.0))))
        density = jnp.exp(-0.5 * u * u) * (1.0 / math.sqrt(2.0 * math.pi))
        g_s[mine, :] = (u * cdf).astype(BF16)
        sl_s[mine, :] = cdf + u * density
        for part in range(2):
            cols = half_cols(part)
            y_send[F_SUM, p, :, cols] = product(g_s[mine, :], w2[:, cols]).astype(BF16)
            y_copy(F_SUM, p, part).start()

    def norm_two(p):
        mine = pair_rows(p)
        h1 = n1_s[mine, :] * gain1 + shift1
        summed = h1 + (y_sum(F_SUM, p) + b_outer)
        centered = summed - row_mean(summed)
        inverse = lax.rsqrt(row_mean(centered * centered) + EPSILON)
        normed = centered * inverse
        mixed_out[mine, :] = (normed * gain2 + shift2).astype(BF16)
        dy = cot[mine, :].astype(F32)
        scaled = dy * gain2
        dz = inverse * (scaled - row_mean(scaled) - normed * row_mean(scaled * normed))
        dz_s[mine, :] = dz
        df_s[mine, :] = dz.astype(BF16)
        add_acc(A_G2, p, fold_rows(dy * normed))
        add_acc(A_S2, p, fold_rows(dy))
        add_acc(A_BOUTER, p, fold_rows(dz))

    def feed_forward_back(p):
        mine = pair_rows(p)
        du = (product(df_s[mine, :], w2[...], 1, 1) * sl_s[mine, :]).astype(BF16)
        du_s[mine, :] = du
        total = fold_rows(du.astype(F32))
        if p == 0:
            accb[...] = total
        else:
            accb[...] = accb[...] + total
        for part in range(2):
            cols = half_cols(part)
            y_send[DH_SUM, p, :, cols] = product(du_s[mine, :], wi[cols, :], 1, 1).astype(BF16)
            y_copy(DH_SUM, p, part).start()

    def norm_one_back(p):
        mine = pair_rows(p)
        dh = dz_s[mine, :] + y_sum(DH_SUM, p)
        normed = n1_s[mine, :]
        scaled = dh * gain1
        dz = r1_s[mine, :] * (scaled - row_mean(scaled) - normed * row_mean(scaled * normed))
        dz_s[mine, :] = dz
        df_s[mine, :] = dz.astype(BF16)
        doc_part_rows = fold_rows(dz[QLEN:, :])
        accx[p] = doc_part_rows
        add_acc(A_G1, p, fold_rows(dh * normed))
        add_acc(A_S1, p, fold_rows(dh))
        add_acc(A_BOUT, p, doc_part_rows + fold_rows(dz[:QLEN, :]))

    def attended_back(p):
        mine = pair_rows(p)
        da_s[mine, :] = product(df_s[mine, :], wo_all[wo_mine, :], 1, 1).astype(BF16)

    def heads_back(p, j):
        mine = pair_rows(p)
        qq, kk, vv = (qkv_s[mine, qkv(kind, j)] for kind in range(3))
        dd = da_s[mine, pl.ds(j * LANES, LANES)]
        low, ds = [], []
        for h in range(2):
            probs = p_s[p * (local // HEAD_DIM) + 2 * j + h]
            low.append(probs.astype(BF16))
            dp = product(head_lanes(dd, h), vv, 1, 1)
            slope = probs * (dp - jnp.sum(probs * dp, axis=1, keepdims=True))
            ds.append(slope.astype(BF16))
        dv = product(jnp.concatenate(low, axis=0), both_heads(dd), 0, 0).astype(BF16)
        dk = product(jnp.concatenate(ds, axis=0), both_heads(qq), 0, 0)
        dq = product(ds[0], head_lanes(kk, 0)) + product(ds[1], head_lanes(kk, 1))
        dq = (dq * 0.125).astype(BF16)
        dqkv_s[mine, qkv(0, j)] = dq
        dqkv_s[mine, qkv(1, j)] = dk.astype(BF16)
        dqkv_s[mine, qkv(2, j)] = dv
        cols = pl.ds(j * LANES, LANES)
        for i, value in enumerate((dq, dv)):
            total = fold_rows(value.astype(F32))
            accq[i, :, cols] = total if p == 0 else accq[i, :, cols] + total

    def attention_back(p):
        attended_back(p)
        for j in range(head_pairs):
            heads_back(p, j)

    def inputs_back(p):
        mine = pair_rows(p)
        part = product(dqkv_s[mine, :], w_qkv[...], 1, 1)
        y_send[DX_SUM, p] = part.astype(BF16)
        accx[p] = jnp.where(t == 0, accx[p], 0.0) + fold_rows(part[QLEN:, :])

    def inputs_send(p):
        for part in range(2):
            y_copy(DX_SUM, p, part).start()

    N_FF = 6
    N_PIECES = 12
    OUT, HEADS, HEADS_MID, HEADS_END, HEADS_LAST, SMALL = range(N_FF, N_PIECES)
    value_split = va0.shape[-1]
    X_Z, Z_X_Z, Z_Z_X = (0, 1, 2, 3), (0, 2, 1, 3), (0, 2, 3, 1)
    HALVING = (X_Z, X_Z, Z_Z_X, X_Z, X_Z, Z_Z_X, X_Z, X_Z, X_Z, X_Z, Z_X_Z, X_Z)

    def piece_refs(m):
        if m < N_FF:
            return [ref.at[m] for ref in (ff0, ff1, ff2, ff3, ff4)]
        if m < HEADS_END:
            return [ref.at[m - N_FF] for ref in (at0, at1, at2, at3, at4)]
        if m == HEADS_END:
            return [va0, va1, va2, va3, va4]
        if m == HEADS_LAST:
            return [vb0, vb1, vb2, vb3, vb4]
        return [ss0, ss1, ss2, ss3, ss4]

    def chunk_index(m, r):
        bits = (r % 2, (r // 2) % 2, (r // 4) % 2, r // 8)
        return tuple(bits[k] for k in HALVING[m])

    def my_index(m):
        return tuple((core, xpos, zlow, zhigh)[k] for k in HALVING[m])

    def piece_copy(m, phase):
        refs = piece_refs(m)
        index = my_index(m)
        peers = (core_peer, x_peer, zlow_peer, zhigh_peer)
        return pltpu.make_async_remote_copy(
            src_ref=refs[0].at[(*index[:phase], 1 - index[phase])],
            dst_ref=refs[phase + 1],
            send_sem=r_ssem.at[m, phase],
            recv_sem=r_rsem.at[m, phase],
            device_id=peers[HALVING[m][phase]],
            device_id_type=MESH,
        )

    def add_piece(mine, index, other, lead):
        if lead == 0:
            value = mine[index].astype(F32) + other[...].astype(F32)
            mine[index] = value.astype(mine.dtype)
            return
        for k in range(2):
            add_piece(mine, (*index, k), other.at[k], lead - 1)

    def advance(m, phase):
        refs = piece_refs(m)
        index = my_index(m)
        piece_copy(m, phase - 1).wait_recv()
        mine, other = refs[0], refs[phase]
        away, stay = 1 - index[phase], index[phase]
        add_piece(mine, (*index[:phase], away), other.at[away], 3 - phase)
        piece_copy(m, phase).start()
        add_piece(mine, (*index[:phase], stay), other.at[stay], 3 - phase)

    def complete(m):
        refs = piece_refs(m)
        index = my_index(m)
        piece_copy(m, 3).wait_recv()
        total = refs[0][index].astype(F32) + refs[4][...].astype(F32)
        if m < N_FF:
            grads_out[m // 3, :, (m % 3) * FF_TILE : (m % 3 + 1) * FF_TILE] = total
        elif m == OUT:
            grads_out[2, :, 0:local] = total
        elif m < SMALL:
            j = min(m - HEADS, 2)
            for k in range(total.shape[1] // LANES):
                kind = k if m < HEADS_LAST else k + value_split // LANES
                first = (1 + kind) * local + j * LANES
                grads_out[2, :, first : first + LANES] = total[:, k * LANES : (k + 1) * LANES]
        else:
            small_out[...] = total

    def weight_grad(m, left, right):
        refs = piece_refs(m)
        grad = product(left, right, 0, 0)
        for r in range(GROUP):
            refs[0][chunk_index(m, r)] = grad[r * chunk : (r + 1) * chunk, :].astype(BF16)
        piece_copy(m, 0).start()

    def outer_grad(n):
        weight_grad(n, df_s[...], g_s[:, n * FF_TILE : (n + 1) * FF_TILE])

    def inner_grad(n):
        weight_grad(3 + n, h1_low[...], du_s[:, n * FF_TILE : (n + 1) * FF_TILE])

    def place_vector(row, eight):
        vector = jnp.sum(eight, axis=0, keepdims=True)
        piece = vector.shape[1] // GROUP
        for r in range(GROUP):
            ss0[(*chunk_index(SMALL, r), slice(row, row + 1), slice(0, piece))] = vector[
                :, r * piece : (r + 1) * piece
            ]

    def heads_grad(m):
        first = (m - HEADS) * group if m < HEADS_LAST else 2 * group + value_split
        last = {HEADS_END: 2 * group + value_split, HEADS_LAST: 3 * group}.get(m, first + group)
        weight_grad(m, x_low[...], dqkv_s[:, first:last])

    def sent_early():
        for copy in out_weight_copies:
            copy.wait_send()
        for p in range(pairs):
            for j in range(local // LANES):
                att_copy(p, j).wait_send()
        doc_steps(doc_sent)

    def sent_late():
        sum_copy.wait_send()
        doc_steps(part_sent)
        for m in range(N_PIECES - 1):
            for phase in range(3 if m < N_FF else 2):
                piece_copy(m, phase).wait_send()

    zero_row = jnp.zeros((1, LANES), F32)
    sum_copy = pltpu.make_async_remote_copy(
        src_ref=sum_send,
        dst_ref=sum_recv,
        send_sem=s_ssem.at[0],
        recv_sem=s_rsem.at[0],
        device_id=y_peer,
        device_id_type=MESH,
    )

    def send_document_sums():
        for p in range(pairs):
            row = jnp.sum(accx[p], axis=0, keepdims=True)
            sum_send[p] = jnp.concatenate(
                [row[:, j * LANES : (j + 1) * LANES] for j in range(doc_cols)]
                + [zero_row] * (8 - doc_cols),
                axis=0,
            )
        sum_copy.start()

    def part_copy(step):
        other = (b + step) % n_batch
        return pltpu.make_async_remote_copy(
            src_ref=doc_part.at[other],
            dst_ref=doc_in.at[b],
            send_sem=d_ssem.at[1, step],
            recv_sem=d_rsem.at[1, b],
            device_id=(other, t),
            device_id_type=MESH,
        )

    def part_arrival(step):
        other = (b + step) % n_batch
        return pltpu.make_async_remote_copy(
            src_ref=doc_part.at[other],
            dst_ref=doc_in.at[other],
            send_sem=d_ssem.at[1, step],
            recv_sem=d_rsem.at[1, other],
            device_id=(other, t),
            device_id_type=MESH,
        )

    def part_start(step, carry):
        part_copy(step).start()
        return carry

    def part_wait(step, carry):
        part_arrival(step).wait_recv()
        return carry

    def part_sent(step, carry):
        part_copy(step).wait_send()
        return carry

    def send_document_parts():
        sum_copy.wait_recv()
        sum_blocks = [sum_send[p] + sum_recv[p] for p in range(pairs)]

        def fill(d, carry):
            for n in range(docs_dev):
                value = jnp.zeros((8, LANES), F32)
                for p in range(pairs):
                    value = value + jnp.where(ids[p] == d * docs_dev + n, sum_blocks[p], 0.0)
                doc_part[d, 8 * n : 8 * n + 8, :] = value
            return carry

        lax.fori_loop(0, n_batch, fill, 0)
        doc_steps(part_start)
        doc_in[b] = doc_part[b]

    def add_document_parts():
        doc_steps(part_wait)

        def add_part(d, total):
            return total + doc_in[d]

        docs_out[...] = lax.fori_loop(0, n_batch, add_part, jnp.zeros(docs_out.shape, F32))

    def input_grad(p):
        y_wait(DX_SUM, p)
        tgrad_out[pair_rows(p), :] = (dz_s[pair_rows(p), :] + y_sum(DX_SUM, p)).astype(BF16)

    make_inputs(0)
    attention(0, 0)
    out_weight_copies[0].wait_recv()
    out_weight_copies[1].start()
    attention(0, 1)
    attention(0, 2)
    make_inputs(1)
    attention(1, 0)
    attention(1, 1)
    out_weight_copies[1].wait_recv()
    out_weight_copies[2].start()
    attention(1, 2)
    wo_load.wait()
    out_weight_copies[2].wait_recv()
    wi_load.wait()
    w2_load.wait()
    attention_out(0)
    feed_forward(0)
    attention_out(1)
    feed_forward(1)
    sent_early()
    cot_load.wait()
    y_wait(F_SUM, 0)
    norm_two(0)
    feed_forward_back(0)
    y_wait(F_SUM, 1)
    norm_two(1)
    outer_grad(1)
    outer_grad(2)
    feed_forward_back(1)
    advance(2, 1)
    inner_grad(1)
    advance(1, 1)
    inner_grad(2)
    advance(5, 1)
    outer_grad(0)
    advance(4, 1)
    inner_grad(0)
    advance(2, 2)
    ss0[...] = jnp.zeros(ss0.shape, F32)
    place_vector(ROW_G2, acc[A_G2])
    place_vector(ROW_S2, acc[A_S2])
    place_vector(ROW_BOUTER, acc[A_BOUTER])
    place_vector(ROW_BIN, accb[...])
    advance(3, 1)
    advance(1, 2)
    y_wait(DH_SUM, 0)
    norm_one_back(0)
    attention_back(0)
    inputs_back(0)
    inputs_send(0)
    advance(5, 2)
    advance(4, 2)
    advance(0, 1)
    y_wait(DH_SUM, 1)
    norm_one_back(1)
    weight_grad(OUT, df_s[...], att_all[:, att_mine])
    advance(1, 3)
    advance(3, 2)
    attended_back(1)
    heads_back(1, 0)
    advance(OUT, 1)
    heads_grad(HEADS)
    advance(4, 3)
    heads_back(1, 1)
    heads_grad(HEADS_MID)
    advance(0, 2)
    advance(HEADS, 1)
    heads_back(1, 2)
    complete(1)
    heads_grad(HEADS_LAST)
    advance(HEADS_MID, 1)
    advance(3, 3)
    advance(HEADS_LAST, 1)
    heads_grad(HEADS_END)
    advance(OUT, 2)
    inputs_back(1)
    send_document_sums()
    inputs_send(1)
    place_vector(ROW_G1, acc[A_G1])
    place_vector(ROW_S1, acc[A_S1])
    place_vector(ROW_BOUT, acc[A_BOUT])
    place_vector(ROW_BQ, accq[0])
    place_vector(ROW_BV, accq[1])
    piece_copy(SMALL, 0).start()
    advance(0, 3)
    advance(SMALL, 1)
    advance(HEADS, 2)
    advance(HEADS_END, 1)
    advance(HEADS_LAST, 2)
    advance(2, 3)
    send_document_parts()
    advance(OUT, 3)
    advance(HEADS_MID, 2)
    advance(SMALL, 2)
    complete(4)
    advance(HEADS, 3)
    complete(3)
    advance(5, 3)
    advance(HEADS_END, 2)
    advance(HEADS_LAST, 3)
    advance(HEADS_MID, 3)
    input_grad(0)
    advance(SMALL, 3)
    complete(5)
    complete(0)
    advance(HEADS_END, 3)
    add_document_parts()
    complete(HEADS_LAST)
    sent_late()
    input_grad(1)
    complete(HEADS_MID)
    complete(2)
    complete(SMALL)
    complete(OUT)
    complete(HEADS)
    complete(HEADS_END)
    for p in range(pairs):
        for part in range(2):
            y_copy(DX_SUM, p, part).wait_send()
            y_copy(F_SUM, p, part).wait_send()
            y_copy(DH_SUM, p, part).wait_send()
    for m in range(N_PIECES):
        for phase in range(3 if m < N_FF else 2 if m < SMALL else 0, 4):
            piece_copy(m, phase).wait_send()


def finish_kernel(
    local, mixed_ref, tgrad_ref, grads_ref, small_ref, docs_ref,
    mixed_out, tgrad_out, doc_out, wq_out, bq_out, wk_out, wv_out, bv_out, wo_out, bo_out,
    g1_out, s1_out, wi_out, bi_out, w2_out, b2_out, g2_out, s2_out,
    out_sem,
):
    moves = [(mixed_ref, mixed_out), (tgrad_ref, tgrad_out), (grads_ref.at[0], w2_out)]
    moves.append((grads_ref.at[1], wi_out))
    for n, target in enumerate((wo_out, wq_out, wk_out, wv_out)):
        moves.append((grads_ref.at[2, :, pl.ds(n * local, local)], target))
    copies = [
        pltpu.make_async_copy(source, target, out_sem.at[i])
        for i, (source, target) in enumerate(moves)
    ]
    for copy in copies:
        copy.start()
    docs_dev, width = doc_out.shape
    for n in range(docs_dev):
        for j in range(width // LANES):
            doc_out[n : n + 1, j * LANES : (j + 1) * LANES] = docs_ref[8 * n + j : 8 * n + j + 1, :]
    for row, out in (
        (ROW_BQ, bq_out), (ROW_BV, bv_out), (ROW_BOUT, bo_out), (ROW_G1, g1_out),
        (ROW_S1, s1_out), (ROW_BIN, bi_out), (ROW_BOUTER, b2_out), (ROW_G2, g2_out),
        (ROW_S2, s2_out),
    ):
        out[...] = small_ref[row, 0 : out.shape[0]]
    for copy in copies:
        copy.wait()


def body(
    n_batch,
    tokens, doc_vectors, doc_ids, w_query, b_query, w_key, w_value, b_value, w_out, b_out,
    gain_one, shift_one, w_inner, b_inner, w_outer, b_outer, gain_two, shift_two, cotangent,
):
    rows, width = tokens.shape
    pairs = doc_ids.shape[0]
    seq = rows // pairs
    local = w_query.shape[1]
    heads = local // HEAD_DIM
    hidden = w_inner.shape[1]
    docs_dev = doc_vectors.shape[0]
    chunk = width // GROUP
    part = hidden // 3
    split = local * 2 // 3 // LANES * LANES
    hbm = pl.BlockSpec(memory_space=pl.ANY)
    vmem = pl.BlockSpec(memory_space=pltpu.VMEM)
    V = pltpu.VMEM
    dma = pltpu.SemaphoreType.DMA
    smalls = (
        b_query, b_value, b_out, gain_one, shift_one, b_inner, b_outer, gain_two, shift_two,
    )
    scratch = [
        V(doc_vectors.shape, BF16), pltpu.SMEM(doc_ids.shape, jnp.int32),
        *[V(item.shape, BF16) for item in smalls],
        V((rows, width), BF16), V((rows, width), BF16),
        V((width, 3 * local), BF16), V((width, width), BF16), V((width, hidden), BF16), V((hidden, width), BF16),
        V((rows, width), BF16),
        V((rows, 3 * local), BF16),
        V((pairs * heads, seq, seq), F32),
        V((rows, width), BF16),
        V((rows, width), F32), V((rows, 1), F32), V((rows, width), BF16),
        V((rows, hidden), BF16), V((rows, hidden), F32),
        V((rows, width), F32), V((rows, width), BF16), V((rows, hidden), BF16),
        V((rows, local), BF16), V((rows, 3 * local), BF16),
        V((6, 8, width), F32), V((8, hidden), F32), V((2, 8, local), F32),
        V((pairs, 8, width), F32),
        V((3, pairs, seq, width), BF16), V((3, pairs, seq, width), BF16),
        *[V((6, *(2,) * n, chunk, part), BF16) for n in (4, 3, 2, 1, 0)],
        *[V((3, *(2,) * n, chunk, local), BF16) for n in (4, 3, 2, 1, 0)],
        *[V((*(2,) * n, chunk, split), BF16) for n in (4, 3, 2, 1, 0)],
        *[V((*(2,) * n, chunk, local - split), BF16) for n in (4, 3, 2, 1, 0)],
        *[V((*(2,) * n, SMALL_ROWS, LANES), F32) for n in (4, 3, 2, 1, 0)],
        V((8 * docs_dev, LANES), BF16), V((n_batch, 8 * docs_dev, LANES), BF16),
        V((n_batch, 8 * docs_dev, LANES), F32), V((n_batch, 8 * docs_dev, LANES), F32),
        V((pairs, 8, LANES), F32), V((pairs, 8, LANES), F32),
        dma((3, pairs, 2)), dma((3, pairs, 2)), dma((pairs, local // LANES)),
        dma((pairs, local // LANES)), dma((3,)), dma((3,)), dma((12, 4)), dma((12, 4)),
        dma((2, n_batch)), dma((2, n_batch)), dma((1,)), dma((1,)), dma((25,)),
    ]
    shape = jax.ShapeDtypeStruct
    mixed, tokens_grad, grads, small, docs = pl.pallas_call(
        functools.partial(layer_kernel, (n_batch, pairs, seq)),
        out_shape=(
            V((rows, width), BF16),
            V((rows, width), BF16),
            V((3, chunk, hidden), F32),
            V((SMALL_ROWS, LANES), F32),
            V((8 * docs_dev, LANES), F32),
        ),
        in_specs=[hbm] * 19,
        out_specs=(vmem,) * 5,
        scratch_shapes=scratch,
        compiler_params=pltpu.CompilerParams(
            collective_id=0, has_side_effects=True, vmem_limit_bytes=60 * 1024 * 1024
        ),
        name="encoder_layer",
    )(
        tokens, cotangent, w_query, w_key, w_value, w_out, w_inner, w_outer,
        doc_vectors, doc_ids, *smalls,
    )

    inner = n_batch // GROUP
    if inner > 1:
        groups = [[g * inner + i for i in range(inner)] for g in range(GROUP)]
        grads = lax.psum_scatter(
            grads, "batch", scatter_dimension=1, axis_index_groups=groups, tiled=True
        )
        small = lax.psum(small, "batch", axis_index_groups=groups)
        part = lax.axis_index("batch") % inner
        pieces = []
        for row in range(SMALL_ROWS):
            wide = {ROW_BQ: local, ROW_BV: local, ROW_BIN: hidden}.get(row, width)
            size = wide // n_batch
            piece = lax.dynamic_slice(small[row], (part * size,), (size,))
            pieces.append(jnp.pad(piece, (0, LANES - size)))
        small = jnp.stack(pieces)

    if inner == 1:
        mixed, tokens_grad, grads, small, docs = (
            pltpu.with_memory_space_constraint(item, pltpu.VMEM)
            for item in (mixed, tokens_grad, grads, small, docs)
        )
    out_rows = width // n_batch
    vector = shape((out_rows,), F32)
    vector_local = shape((local // n_batch,), F32)
    square = shape((out_rows, local), F32)
    (
        mixed, tokens_grad, doc_grad, wq_grad, bq_grad, wk_grad, wv_grad, bv_grad, wo_grad, bo_grad, g1_grad, s1_grad,
        wi_grad, bi_grad, w2_grad, b2_grad, g2_grad, s2_grad,
    ) = pl.pallas_call(
        functools.partial(finish_kernel, local),
        out_shape=(
            shape((rows, width), BF16), shape((rows, width), BF16),
            shape((docs_dev, width), F32), square, vector_local, square, square, vector_local,
            square, vector, vector, vector,
            shape((out_rows, hidden), F32), shape((hidden // n_batch,), F32),
            shape((out_rows, hidden), F32), vector, vector, vector,
        ),
        in_specs=[vmem] * 5,
        out_specs=(
            hbm, hbm, vmem, hbm, vmem, hbm, hbm, vmem, hbm, vmem, vmem, vmem, hbm, vmem, hbm,
            vmem, vmem, vmem,
        ),
        scratch_shapes=[dma((8,))],
        name="gradient_outputs",
    )(mixed, tokens_grad, grads, small, docs)
    return (
        mixed, tokens_grad, doc_grad, wq_grad, bq_grad, wk_grad, wv_grad, bv_grad, wo_grad.T,
        bo_grad, g1_grad, s1_grad, wi_grad, bi_grad, w2_grad.T, b2_grad, g2_grad, s2_grad,
    )


def solution(mesh):
    in_specs = (
        P("batch", None), P("batch", None), P("batch"), P(None, "tensor"), P("tensor"),
        P(None, "tensor"), P(None, "tensor"), P("tensor"), P("tensor", None), P(), P(), P(),
        P(None, "tensor"), P("tensor"), P("tensor", None), P(), P(), P(), P("batch", None),
    )
    out_specs = (
        P("batch", None), P("batch", None), P("batch", None), P("batch", "tensor"),
        P(("tensor", "batch")), P("batch", "tensor"), P("batch", "tensor"),
        P(("tensor", "batch")), P("tensor", "batch"), P("batch"), P("batch"), P("batch"),
        P("batch", "tensor"), P(("tensor", "batch")), P("tensor", "batch"), P("batch"),
        P("batch"), P("batch"),
    )
    return jax.shard_map(
        functools.partial(body, mesh.shape["batch"]),
        mesh=mesh, in_specs=in_specs, out_specs=out_specs, check_vma=False,
    )
```

```python
import functools
import math

import jax
import jax.numpy as jnp
from jax import lax
from jax.experimental import pallas as pl
from jax.experimental.pallas import tpu as pltpu
from jax.sharding import PartitionSpec as P

HEAD_DIM = 64
QLEN = 32
LANES = 128
GROUP = 16
EPSILON = 1e-12
F32 = jnp.float32
BF16 = jnp.bfloat16
MESH = pl.DeviceIdType.MESH

ROW_BQ, ROW_BV, ROW_BOUT, ROW_G1, ROW_S1, ROW_BIN, ROW_BOUTER, ROW_G2, ROW_S2 = range(9)
SMALL_ROWS = 16


def product(left, right, left_dim=1, right_dim=0):
    return lax.dot_general(
        left, right, (((left_dim,), (right_dim,)), ((), ())), preferred_element_type=F32
    )


def fold_rows(block):
    return jnp.sum(block.reshape(block.shape[0] // 8, 8, block.shape[1]), axis=0)


def row_mean(block):
    return jnp.mean(block, axis=1, keepdims=True)


def layer_kernel(
    sizes,
    tokens_hbm, cot_hbm, wq_hbm, wk_hbm, wv_hbm, wo_hbm, wi_hbm, w2_hbm,
    docs_hbm, ids_hbm, bq_hbm, bv_hbm, bo_hbm, g1_hbm, s1_hbm, bi_hbm, b2_hbm, g2_hbm, s2_hbm,
    mixed_out, tgrad_out, grads_out, small_out, docs_out,
    docs_ref, ids_ref, bq_ref, bv_ref, bo_ref, g1_ref, s1_ref, bi_ref, b2_ref, g2_ref, s2_ref,
    tok, cot, w_qkv, wo_all, wi, w2,
    x_low, qkv_s, p_s, att_all, n1_s, r1_s, h1_low, g_s, sl_s, dz_s, df_s, du_s,
    da_s, dqkv_s, acc, accb, accq, accx,
    y_send, y_recv, ff0, ff1, ff2, ff3, ff4, at0, at1, at2, at3, at4,
    va0, va1, va2, va3, va4, vb0, vb1, vb2, vb3, vb4, ss0, ss1, ss2, ss3, ss4,
    doc_stage, doc_table, doc_part, doc_in, sum_send, sum_recv,
    y_ssem, y_rsem, a_ssem, a_rsem, w_ssem, w_rsem, r_ssem, r_rsem, d_ssem, d_rsem,
    s_ssem, s_rsem, load_sem,
):
    n_batch, pairs, seq = sizes
    rows, width = tok.shape
    local = wq_hbm.shape[1]
    hidden = wi.shape[1]
    chunk = width // GROUP
    docs_dev = docs_ref.shape[0]
    doc_cols = width // LANES
    inner = n_batch // GROUP

    b = lax.axis_index("batch")
    t = lax.axis_index("tensor")
    place = b // inner
    rest = b % inner
    core = place % 2
    xpos = (place // 2) % 2
    zlow = (place // 4) % 2
    zhigh = place // 8

    def at_place(other):
        return (other * inner + rest, t)

    y_peer = (b, 1 - t)
    core_peer = at_place(place + 1 - 2 * core)
    x_peer = at_place(place + 2 - 4 * xpos)
    zlow_peer = at_place(place + 4 - 8 * zlow)
    zhigh_peer = at_place(place + 8 - 16 * zhigh)

    def batch_peer(step):
        return ((b + step) % n_batch, t)

    def doc_steps(step):
        if n_batch <= GROUP:
            for i in range(1, n_batch):
                step(i, 0)
        else:
            lax.fori_loop(1, n_batch, step, 0)

    barrier = pltpu.get_barrier_semaphore()

    def greet(step, carry):
        pl.semaphore_signal(barrier, inc=1, device_id=batch_peer(step), device_id_type=MESH)
        return carry

    doc_steps(greet)
    pl.semaphore_signal(barrier, inc=1, device_id=y_peer, device_id_type=MESH)

    wo_mine = pl.ds(pl.multiple_of(t * local, LANES), local)
    att_mine = wo_mine
    loads = []
    vectors = (
        (bq_hbm, bq_ref), (bv_hbm, bv_ref), (bo_hbm, bo_ref), (g1_hbm, g1_ref), (s1_hbm, s1_ref),
        (bi_hbm, bi_ref), (b2_hbm, b2_ref), (g2_hbm, g2_ref), (s2_hbm, s2_ref),
    )
    head_pairs = local // LANES
    group = 3 * LANES
    qkv_weights = [
        (
            source.at[:, pl.ds(j * LANES, LANES)],
            w_qkv.at[:, pl.ds(j * group + kind * LANES, LANES)],
        )
        for j in range(head_pairs)
        for kind, source in enumerate((wq_hbm, wk_hbm, wv_hbm))
    ]
    for i, (src, dst) in enumerate(
        (
            (docs_hbm, docs_ref), (ids_hbm, ids_ref), *vectors,
            (tokens_hbm, tok), *qkv_weights,
            (wo_hbm, wo_all.at[wo_mine]), (wi_hbm, wi), (w2_hbm, w2), (cot_hbm, cot),
        )
    ):
        copy = pltpu.make_async_copy(src, dst, load_sem.at[i])
        copy.start()
        loads.append(copy)
    docs_load, ids_load = loads[:2]
    tok_load, *qkv_loads = loads[2 + len(vectors) : -4]
    wo_load, wi_load, w2_load, cot_load = loads[-4:]
    docs_load.wait()

    doc_rows = docs_ref[...].astype(F32)
    pieces = []
    for n in range(docs_dev):
        for j in range(8):
            if j < doc_cols:
                pieces.append(doc_rows[n : n + 1, j * LANES : (j + 1) * LANES])
            else:
                pieces.append(jnp.zeros((1, LANES), F32))
    stage = jnp.concatenate(pieces, axis=0).astype(BF16)
    doc_stage[...] = stage
    doc_table[b] = stage

    pl.semaphore_wait(barrier, n_batch)

    share = local // 4

    def share_rows(tensor, first, count):
        start = tensor * local + first * share
        return pl.ds(pl.multiple_of(start, 16), count * share)

    quarter = 2 * core + xpos
    out_weight_copies = [
        pltpu.make_async_remote_copy(
            src_ref=source,
            dst_ref=wo_all.at[target],
            send_sem=w_ssem.at[i],
            recv_sem=w_rsem.at[i],
            device_id=peer,
            device_id_type=MESH,
        )
        for i, (source, target, peer) in enumerate(
            (
                (
                    wo_hbm.at[pl.ds(pl.multiple_of(quarter * share, 16), share)],
                    share_rows(t, quarter, 1),
                    y_peer,
                ),
                (
                    wo_all.at[share_rows(1 - t, quarter, 1)],
                    share_rows(1 - t, quarter, 1),
                    x_peer,
                ),
                (
                    wo_all.at[share_rows(1 - t, 2 * core, 2)],
                    share_rows(1 - t, 2 * core, 2),
                    core_peer,
                ),
            )
        )
    ]
    out_weight_copies[0].start()

    def doc_copy(step):
        return pltpu.make_async_remote_copy(
            src_ref=doc_stage,
            dst_ref=doc_table.at[b],
            send_sem=d_ssem.at[0, step],
            recv_sem=d_rsem.at[0, b],
            device_id=batch_peer(step),
            device_id_type=MESH,
        )

    def doc_arrival(step):
        other = (b + step) % n_batch
        return pltpu.make_async_remote_copy(
            src_ref=doc_stage,
            dst_ref=doc_table.at[other],
            send_sem=d_ssem.at[0, step],
            recv_sem=d_rsem.at[0, other],
            device_id=batch_peer(step),
            device_id_type=MESH,
        )

    def doc_start(step, carry):
        doc_copy(step).start()
        return carry

    def doc_wait(step, carry):
        doc_arrival(step).wait_recv()
        return carry

    def doc_sent(step, carry):
        doc_copy(step).wait_send()
        return carry

    doc_steps(doc_start)

    for copy in loads[2 : 2 + len(vectors)]:
        copy.wait()
    b_query = bq_ref[...].astype(F32).reshape(1, local)
    b_value = bv_ref[...].astype(F32).reshape(1, local)
    b_out = bo_ref[...].astype(F32).reshape(1, width)
    gain1 = g1_ref[...].astype(F32).reshape(1, width)
    shift1 = s1_ref[...].astype(F32).reshape(1, width)
    b_inner = bi_ref[...].astype(F32).reshape(1, hidden)
    b_outer = b2_ref[...].astype(F32).reshape(1, width)
    gain2 = g2_ref[...].astype(F32).reshape(1, width)
    shift2 = s2_ref[...].astype(F32).reshape(1, width)

    tok_load.wait()
    doc_steps(doc_wait)

    ids_load.wait()
    ids = [jnp.full((8, LANES), ids_ref[p], jnp.int32) for p in range(pairs)]

    def pick(d, found):
        block = doc_table[d].astype(F32)
        result = []
        for p in range(pairs):
            value = found[p]
            for n in range(docs_dev):
                value = value + jnp.where(
                    ids[p] == d * docs_dev + n, block[8 * n : 8 * n + 8, :], 0.0
                )
            result.append(value)
        return tuple(result)

    found = lax.fori_loop(
        0, n_batch, pick, tuple(jnp.zeros((8, LANES), F32) for _ in range(pairs))
    )
    doc_row = [
        jnp.concatenate([found[p][j : j + 1, :] for j in range(doc_cols)], axis=1)
        for p in range(pairs)
    ]

    def pair_rows(p):
        return pl.ds(p * seq, seq)

    def inputs_of(p):
        where_row = lax.broadcasted_iota(jnp.int32, (seq, 1), 0)
        return tok[pair_rows(p), :].astype(F32) + jnp.where(where_row >= QLEN, doc_row[p], 0.0)

    half = width // 2

    def half_cols(part):
        return pl.ds(part * half, half)

    def y_copy(kind, p, part):
        return pltpu.make_async_remote_copy(
            src_ref=y_send.at[kind, p, :, half_cols(part)],
            dst_ref=y_recv.at[kind, p, :, half_cols(part)],
            send_sem=y_ssem.at[kind, p, part],
            recv_sem=y_rsem.at[kind, p, part],
            device_id=y_peer,
            device_id_type=MESH,
        )

    def y_wait(kind, p):
        for part in range(2):
            y_copy(kind, p, part).wait_recv()

    def y_sum(kind, p):
        return y_send[kind, p].astype(F32) + y_recv[kind, p].astype(F32)

    F_SUM, DH_SUM, DX_SUM = range(3)

    def att_cols(tensor, j):
        return pl.ds(pl.multiple_of(tensor * local + j * LANES, LANES), LANES)

    def att_copy(p, j):
        place_of = att_all.at[pair_rows(p), att_cols(t, j)]
        return pltpu.make_async_remote_copy(
            src_ref=place_of,
            dst_ref=place_of,
            send_sem=a_ssem.at[p, j],
            recv_sem=a_rsem.at[p, j],
            device_id=y_peer,
            device_id_type=MESH,
        )

    first_lanes = lax.broadcasted_iota(jnp.int32, (1, LANES), 1) < HEAD_DIM

    def head_lanes(values, h):
        keep = first_lanes if h == 0 else jnp.logical_not(first_lanes)
        return jnp.where(keep, values, jnp.zeros_like(values))

    def both_heads(values):
        return jnp.concatenate([head_lanes(values, 0), head_lanes(values, 1)], axis=0)

    def add_acc(which, p, value):
        if p == 0:
            acc[which] = value
        else:
            acc[which] = acc[which] + value

    A_G2, A_S2, A_BOUTER, A_G1, A_S1, A_BOUT = range(6)

    def project(p):
        mine = pair_rows(p)
        x_low[mine, :] = inputs_of(p).astype(BF16)
        qkv_s[mine, :] = (product(x_low[mine, :], w_qkv[...]) + b_qkv).astype(BF16)

    def qkv(kind, j):
        return pl.ds(j * group + kind * LANES, LANES)

    def make_inputs(p):
        x_low[pair_rows(p), :] = inputs_of(p).astype(BF16)

    def attention(p, j):
        mine = pair_rows(p)
        here = pl.ds(j * LANES, LANES)
        if p == 0:
            for copy in qkv_loads[3 * j : 3 * j + 3]:
                copy.wait()
        both = product(x_low[mine, :], w_qkv[:, pl.ds(j * group, group)])
        qq = (both[:, 0:LANES] + b_query[:, j * LANES : (j + 1) * LANES]).astype(BF16)
        qq = (qq.astype(F32) * 0.125).astype(BF16)
        kk = both[:, LANES : 2 * LANES].astype(BF16)
        vv = (both[:, 2 * LANES :] + b_value[:, j * LANES : (j + 1) * LANES]).astype(BF16)
        qkv_s[mine, qkv(0, j)] = qq
        qkv_s[mine, qkv(1, j)] = kk
        qkv_s[mine, qkv(2, j)] = vv
        low = []
        for h in range(2):
            scores = product(head_lanes(qq, h), kk, 1, 1)
            expo = jnp.exp(scores - jnp.max(scores, axis=1, keepdims=True))
            probs = expo * (1.0 / jnp.sum(expo, axis=1, keepdims=True))
            p_s[p * (local // HEAD_DIM) + 2 * j + h] = probs
            low.append(probs.astype(BF16))
        out = product(low[0], head_lanes(vv, 0)) + product(low[1], head_lanes(vv, 1))
        att_all[mine, att_cols(t, j)] = out.astype(BF16)
        att_copy(p, j).start()

    def attention_out(p):
        for j in range(local // LANES):
            att_copy(p, j).wait_recv()
        mine = pair_rows(p)
        summed = inputs_of(p) + (product(att_all[mine, :], wo_all[...]) + b_out)
        centered = summed - row_mean(summed)
        inverse = lax.rsqrt(row_mean(centered * centered) + EPSILON)
        normed = centered * inverse
        n1_s[mine, :] = normed
        r1_s[mine, :] = inverse
        h1_low[mine, :] = (normed * gain1 + shift1).astype(BF16)

    FF_TILE = 512

    def feed_forward(p):
        mine = pair_rows(p)
        u = product(h1_low[mine, :], wi[...]) + b_inner
        cdf = 0.5 * (1.0 + lax.erf(u * (1.0 / math.sqrt(2.0))))
        density = jnp.exp(-0.5 * u * u) * (1.0 / math.sqrt(2.0 * math.pi))
        g_s[mine, :] = (u * cdf).astype(BF16)
        sl_s[mine, :] = cdf + u * density
        for part in range(2):
            cols = half_cols(part)
            y_send[F_SUM, p, :, cols] = product(g_s[mine, :], w2[:, cols]).astype(BF16)
            y_copy(F_SUM, p, part).start()

    def norm_two(p):
        mine = pair_rows(p)
        h1 = n1_s[mine, :] * gain1 + shift1
        summed = h1 + (y_sum(F_SUM, p) + b_outer)
        centered = summed - row_mean(summed)
        inverse = lax.rsqrt(row_mean(centered * centered) + EPSILON)
        normed = centered * inverse
        mixed_out[mine, :] = (normed * gain2 + shift2).astype(BF16)
        dy = cot[mine, :].astype(F32)
        scaled = dy * gain2
        dz = inverse * (scaled - row_mean(scaled) - normed * row_mean(scaled * normed))
        dz_s[mine, :] = dz
        df_s[mine, :] = dz.astype(BF16)
        add_acc(A_G2, p, fold_rows(dy * normed))
        add_acc(A_S2, p, fold_rows(dy))
        add_acc(A_BOUTER, p, fold_rows(dz))

    def feed_forward_back(p):
        mine = pair_rows(p)
        du = (product(df_s[mine, :], w2[...], 1, 1) * sl_s[mine, :]).astype(BF16)
        du_s[mine, :] = du
        total = fold_rows(du.astype(F32))
        if p == 0:
            accb[...] = total
        else:
            accb[...] = accb[...] + total
        for part in range(2):
            cols = half_cols(part)
            y_send[DH_SUM, p, :, cols] = product(du_s[mine, :], wi[cols, :], 1, 1).astype(BF16)
            y_copy(DH_SUM, p, part).start()

    def norm_one_back(p):
        mine = pair_rows(p)
        dh = dz_s[mine, :] + y_sum(DH_SUM, p)
        normed = n1_s[mine, :]
        scaled = dh * gain1
        dz = r1_s[mine, :] * (scaled - row_mean(scaled) - normed * row_mean(scaled * normed))
        dz_s[mine, :] = dz
        df_s[mine, :] = dz.astype(BF16)
        doc_part_rows = fold_rows(dz[QLEN:, :])
        accx[p] = doc_part_rows
        add_acc(A_G1, p, fold_rows(dh * normed))
        add_acc(A_S1, p, fold_rows(dh))
        add_acc(A_BOUT, p, doc_part_rows + fold_rows(dz[:QLEN, :]))

    def attended_back(p):
        mine = pair_rows(p)
        da_s[mine, :] = product(df_s[mine, :], wo_all[wo_mine, :], 1, 1).astype(BF16)

    def heads_back(p, j):
        mine = pair_rows(p)
        qq, kk, vv = (qkv_s[mine, qkv(kind, j)] for kind in range(3))
        dd = da_s[mine, pl.ds(j * LANES, LANES)]
        low, ds = [], []
        for h in range(2):
            probs = p_s[p * (local // HEAD_DIM) + 2 * j + h]
            low.append(probs.astype(BF16))
            dp = product(head_lanes(dd, h), vv, 1, 1)
            slope = probs * (dp - jnp.sum(probs * dp, axis=1, keepdims=True))
            ds.append(slope.astype(BF16))
        dv = product(jnp.concatenate(low, axis=0), both_heads(dd), 0, 0).astype(BF16)
        dk = product(jnp.concatenate(ds, axis=0), both_heads(qq), 0, 0)
        dq = product(ds[0], head_lanes(kk, 0)) + product(ds[1], head_lanes(kk, 1))
        dq = (dq * 0.125).astype(BF16)
        dqkv_s[mine, qkv(0, j)] = dq
        dqkv_s[mine, qkv(1, j)] = dk.astype(BF16)
        dqkv_s[mine, qkv(2, j)] = dv
        cols = pl.ds(j * LANES, LANES)
        for i, value in enumerate((dq, dv)):
            total = fold_rows(value.astype(F32))
            accq[i, :, cols] = total if p == 0 else accq[i, :, cols] + total

    def attention_back(p):
        attended_back(p)
        for j in range(head_pairs):
            heads_back(p, j)

    def inputs_back(p):
        mine = pair_rows(p)
        part = product(dqkv_s[mine, :], w_qkv[...], 1, 1)
        y_send[DX_SUM, p] = part.astype(BF16)
        accx[p] = jnp.where(t == 0, accx[p], 0.0) + fold_rows(part[QLEN:, :])

    def inputs_send(p):
        for part in range(2):
            y_copy(DX_SUM, p, part).start()

    N_FF = 6
    N_PIECES = 12
    OUT, HEADS, HEADS_MID, HEADS_END, HEADS_LAST, SMALL = range(N_FF, N_PIECES)
    value_split = va0.shape[-1]
    X_Z, Z_X_Z, Z_Z_X = (0, 1, 2, 3), (0, 2, 1, 3), (0, 2, 3, 1)
    HALVING = (X_Z, X_Z, Z_Z_X, X_Z, Z_Z_X, X_Z, X_Z, X_Z, X_Z, X_Z, Z_X_Z, X_Z)

    def piece_refs(m):
        if m < N_FF:
            return [ref.at[m] for ref in (ff0, ff1, ff2, ff3, ff4)]
        if m < HEADS_END:
            return [ref.at[m - N_FF] for ref in (at0, at1, at2, at3, at4)]
        if m == HEADS_END:
            return [va0, va1, va2, va3, va4]
        if m == HEADS_LAST:
            return [vb0, vb1, vb2, vb3, vb4]
        return [ss0, ss1, ss2, ss3, ss4]

    def chunk_index(m, r):
        bits = (r % 2, (r // 2) % 2, (r // 4) % 2, r // 8)
        return tuple(bits[k] for k in HALVING[m])

    def my_index(m):
        return tuple((core, xpos, zlow, zhigh)[k] for k in HALVING[m])

    def piece_copy(m, phase):
        refs = piece_refs(m)
        index = my_index(m)
        peers = (core_peer, x_peer, zlow_peer, zhigh_peer)
        return pltpu.make_async_remote_copy(
            src_ref=refs[0].at[(*index[:phase], 1 - index[phase])],
            dst_ref=refs[phase + 1],
            send_sem=r_ssem.at[m, phase],
            recv_sem=r_rsem.at[m, phase],
            device_id=peers[HALVING[m][phase]],
            device_id_type=MESH,
        )

    def add_piece(mine, index, other, lead):
        if lead == 0:
            value = mine[index].astype(F32) + other[...].astype(F32)
            mine[index] = value.astype(mine.dtype)
            return
        for k in range(2):
            add_piece(mine, (*index, k), other.at[k], lead - 1)

    def advance(m, phase):
        refs = piece_refs(m)
        index = my_index(m)
        piece_copy(m, phase - 1).wait_recv()
        mine, other = refs[0], refs[phase]
        away, stay = 1 - index[phase], index[phase]
        add_piece(mine, (*index[:phase], away), other.at[away], 3 - phase)
        piece_copy(m, phase).start()
        add_piece(mine, (*index[:phase], stay), other.at[stay], 3 - phase)

    def complete(m):
        refs = piece_refs(m)
        index = my_index(m)
        piece_copy(m, 3).wait_recv()
        total = refs[0][index].astype(F32) + refs[4][...].astype(F32)
        if m < N_FF:
            grads_out[m // 3, :, (m % 3) * FF_TILE : (m % 3 + 1) * FF_TILE] = total
        elif m == OUT:
            grads_out[2, :, 0:local] = total
        elif m < SMALL:
            j = min(m - HEADS, 2)
            for k in range(total.shape[1] // LANES):
                kind = k if m < HEADS_LAST else k + value_split // LANES
                first = (1 + kind) * local + j * LANES
                grads_out[2, :, first : first + LANES] = total[:, k * LANES : (k + 1) * LANES]
        else:
            small_out[...] = total

    def weight_grad(m, left, right):
        refs = piece_refs(m)
        grad = product(left, right, 0, 0)
        for r in range(GROUP):
            refs[0][chunk_index(m, r)] = grad[r * chunk : (r + 1) * chunk, :].astype(BF16)
        piece_copy(m, 0).start()

    def outer_grad(n):
        weight_grad(n, df_s[...], g_s[:, n * FF_TILE : (n + 1) * FF_TILE])

    def inner_grad(n):
        weight_grad(3 + n, h1_low[...], du_s[:, n * FF_TILE : (n + 1) * FF_TILE])

    def place_vector(row, eight):
        vector = jnp.sum(eight, axis=0, keepdims=True)
        piece = vector.shape[1] // GROUP
        for r in range(GROUP):
            ss0[(*chunk_index(SMALL, r), slice(row, row + 1), slice(0, piece))] = vector[
                :, r * piece : (r + 1) * piece
            ]

    def heads_grad(m):
        first = (m - HEADS) * group if m < HEADS_LAST else 2 * group + value_split
        last = {HEADS_END: 2 * group + value_split, HEADS_LAST: 3 * group}.get(m, first + group)
        weight_grad(m, x_low[...], dqkv_s[:, first:last])

    def sent_early():
        for copy in out_weight_copies:
            copy.wait_send()
        for p in range(pairs):
            for j in range(local // LANES):
                att_copy(p, j).wait_send()
        doc_steps(doc_sent)

    def sent_late():
        sum_copy.wait_send()
        doc_steps(part_sent)
        for m in range(N_PIECES - 1):
            for phase in range(3 if m < N_FF else 2):
                piece_copy(m, phase).wait_send()

    zero_row = jnp.zeros((1, LANES), F32)
    sum_copy = pltpu.make_async_remote_copy(
        src_ref=sum_send,
        dst_ref=sum_recv,
        send_sem=s_ssem.at[0],
        recv_sem=s_rsem.at[0],
        device_id=y_peer,
        device_id_type=MESH,
    )

    def send_document_sums():
        for p in range(pairs):
            row = jnp.sum(accx[p], axis=0, keepdims=True)
            sum_send[p] = jnp.concatenate(
                [row[:, j * LANES : (j + 1) * LANES] for j in range(doc_cols)]
                + [zero_row] * (8 - doc_cols),
                axis=0,
            )
        sum_copy.start()

    def part_copy(step):
        other = (b + step) % n_batch
        return pltpu.make_async_remote_copy(
            src_ref=doc_part.at[other],
            dst_ref=doc_in.at[b],
            send_sem=d_ssem.at[1, step],
            recv_sem=d_rsem.at[1, b],
            device_id=(other, t),
            device_id_type=MESH,
        )

    def part_arrival(step):
        other = (b + step) % n_batch
        return pltpu.make_async_remote_copy(
            src_ref=doc_part.at[other],
            dst_ref=doc_in.at[other],
            send_sem=d_ssem.at[1, step],
            recv_sem=d_rsem.at[1, other],
            device_id=(other, t),
            device_id_type=MESH,
        )

    def part_start(step, carry):
        part_copy(step).start()
        return carry

    def part_wait(step, carry):
        part_arrival(step).wait_recv()
        return carry

    def part_sent(step, carry):
        part_copy(step).wait_send()
        return carry

    def send_document_parts():
        sum_copy.wait_recv()
        sum_blocks = [sum_send[p] + sum_recv[p] for p in range(pairs)]

        def fill(d, carry):
            for n in range(docs_dev):
                value = jnp.zeros((8, LANES), F32)
                for p in range(pairs):
                    value = value + jnp.where(ids[p] == d * docs_dev + n, sum_blocks[p], 0.0)
                doc_part[d, 8 * n : 8 * n + 8, :] = value
            return carry

        lax.fori_loop(0, n_batch, fill, 0)
        doc_steps(part_start)
        doc_in[b] = doc_part[b]

    def add_document_parts():
        doc_steps(part_wait)

        def add_part(d, total):
            return total + doc_in[d]

        docs_out[...] = lax.fori_loop(0, n_batch, add_part, jnp.zeros(docs_out.shape, F32))

    def input_grad(p):
        y_wait(DX_SUM, p)
        tgrad_out[pair_rows(p), :] = (dz_s[pair_rows(p), :] + y_sum(DX_SUM, p)).astype(BF16)

    make_inputs(0)
    attention(0, 0)
    out_weight_copies[0].wait_recv()
    out_weight_copies[1].start()
    attention(0, 1)
    attention(0, 2)
    make_inputs(1)
    attention(1, 0)
    attention(1, 1)
    attention(1, 2)
    out_weight_copies[1].wait_recv()
    out_weight_copies[2].start()
    wo_load.wait()
    out_weight_copies[2].wait_recv()
    wi_load.wait()
    w2_load.wait()
    attention_out(0)
    feed_forward(0)
    attention_out(1)
    feed_forward(1)
    sent_early()
    cot_load.wait()
    y_wait(F_SUM, 0)
    norm_two(0)
    feed_forward_back(0)
    y_wait(F_SUM, 1)
    norm_two(1)
    outer_grad(2)
    outer_grad(1)
    advance(2, 1)
    feed_forward_back(1)
    advance(1, 1)
    inner_grad(1)
    inner_grad(2)
    outer_grad(0)
    advance(4, 1)
    ss0[...] = jnp.zeros(ss0.shape, F32)
    place_vector(ROW_G2, acc[A_G2])
    place_vector(ROW_S2, acc[A_S2])
    place_vector(ROW_BOUTER, acc[A_BOUTER])
    place_vector(ROW_BIN, accb[...])
    advance(5, 1)
    inner_grad(0)
    advance(0, 1)
    advance(2, 2)
    y_wait(DH_SUM, 0)
    norm_one_back(0)
    attention_back(0)
    inputs_back(0)
    inputs_send(0)
    advance(1, 2)
    advance(3, 1)
    advance(4, 2)
    advance(5, 2)
    y_wait(DH_SUM, 1)
    norm_one_back(1)
    weight_grad(OUT, df_s[...], att_all[:, att_mine])
    advance(1, 3)
    advance(0, 2)
    attended_back(1)
    heads_back(1, 0)
    advance(OUT, 1)
    heads_grad(HEADS)
    heads_back(1, 1)
    advance(5, 3)
    heads_back(1, 2)
    advance(3, 2)
    advance(HEADS, 1)
    heads_grad(HEADS_LAST)
    heads_grad(HEADS_MID)
    place_vector(ROW_G1, acc[A_G1])
    place_vector(ROW_S1, acc[A_S1])
    place_vector(ROW_BOUT, acc[A_BOUT])
    place_vector(ROW_BQ, accq[0])
    place_vector(ROW_BV, accq[1])
    piece_copy(SMALL, 0).start()
    complete(1)
    advance(HEADS_LAST, 1)
    advance(0, 3)
    advance(HEADS_MID, 1)
    advance(OUT, 2)
    advance(SMALL, 1)
    heads_grad(HEADS_END)
    complete(5)
    inputs_back(1)
    send_document_sums()
    inputs_send(1)
    advance(HEADS_END, 1)
    advance(3, 3)
    advance(HEADS, 2)
    send_document_parts()
    advance(HEADS_LAST, 2)
    advance(OUT, 3)
    advance(HEADS_MID, 2)
    complete(0)
    advance(SMALL, 2)
    advance(4, 3)
    advance(HEADS, 3)
    advance(HEADS_END, 2)
    advance(HEADS_LAST, 3)
    advance(HEADS_MID, 3)
    advance(2, 3)
    complete(OUT)
    advance(SMALL, 3)
    complete(3)
    advance(HEADS_END, 3)
    input_grad(0)
    add_document_parts()
    complete(HEADS)
    sent_late()
    input_grad(1)
    complete(HEADS_LAST)
    complete(HEADS_MID)
    complete(4)
    complete(SMALL)
    complete(2)
    complete(HEADS_END)
    for p in range(pairs):
        for part in range(2):
            y_copy(DX_SUM, p, part).wait_send()
            y_copy(F_SUM, p, part).wait_send()
            y_copy(DH_SUM, p, part).wait_send()
    for m in range(N_PIECES):
        for phase in range(3 if m < N_FF else 2 if m < SMALL else 0, 4):
            piece_copy(m, phase).wait_send()


def finish_kernel(
    local, mixed_ref, tgrad_ref, grads_ref, small_ref, docs_ref,
    mixed_out, tgrad_out, doc_out, wq_out, bq_out, wk_out, wv_out, bv_out, wo_out, bo_out,
    g1_out, s1_out, wi_out, bi_out, w2_out, b2_out, g2_out, s2_out,
    out_sem,
):
    moves = [(mixed_ref, mixed_out), (tgrad_ref, tgrad_out), (grads_ref.at[0], w2_out)]
    moves.append((grads_ref.at[1], wi_out))
    for n, target in enumerate((wo_out, wq_out, wk_out, wv_out)):
        moves.append((grads_ref.at[2, :, pl.ds(n * local, local)], target))
    copies = [
        pltpu.make_async_copy(source, target, out_sem.at[i])
        for i, (source, target) in enumerate(moves)
    ]
    for copy in copies:
        copy.start()
    docs_dev, width = doc_out.shape
    for n in range(docs_dev):
        for j in range(width // LANES):
            doc_out[n : n + 1, j * LANES : (j + 1) * LANES] = docs_ref[8 * n + j : 8 * n + j + 1, :]
    for row, out in (
        (ROW_BQ, bq_out), (ROW_BV, bv_out), (ROW_BOUT, bo_out), (ROW_G1, g1_out),
        (ROW_S1, s1_out), (ROW_BIN, bi_out), (ROW_BOUTER, b2_out), (ROW_G2, g2_out),
        (ROW_S2, s2_out),
    ):
        out[...] = small_ref[row, 0 : out.shape[0]]
    for copy in copies:
        copy.wait()


def body(
    n_batch,
    tokens, doc_vectors, doc_ids, w_query, b_query, w_key, w_value, b_value, w_out, b_out,
    gain_one, shift_one, w_inner, b_inner, w_outer, b_outer, gain_two, shift_two, cotangent,
):
    rows, width = tokens.shape
    pairs = doc_ids.shape[0]
    seq = rows // pairs
    local = w_query.shape[1]
    heads = local // HEAD_DIM
    hidden = w_inner.shape[1]
    docs_dev = doc_vectors.shape[0]
    chunk = width // GROUP
    part = hidden // 3
    split = local * 2 // 3 // LANES * LANES
    hbm = pl.BlockSpec(memory_space=pl.ANY)
    vmem = pl.BlockSpec(memory_space=pltpu.VMEM)
    V = pltpu.VMEM
    dma = pltpu.SemaphoreType.DMA
    smalls = (
        b_query, b_value, b_out, gain_one, shift_one, b_inner, b_outer, gain_two, shift_two,
    )
    scratch = [
        V(doc_vectors.shape, BF16), pltpu.SMEM(doc_ids.shape, jnp.int32),
        *[V(item.shape, BF16) for item in smalls],
        V((rows, width), BF16), V((rows, width), BF16),
        V((width, 3 * local), BF16), V((width, width), BF16), V((width, hidden), BF16), V((hidden, width), BF16),
        V((rows, width), BF16),
        V((rows, 3 * local), BF16),
        V((pairs * heads, seq, seq), F32),
        V((rows, width), BF16),
        V((rows, width), F32), V((rows, 1), F32), V((rows, width), BF16),
        V((rows, hidden), BF16), V((rows, hidden), F32),
        V((rows, width), F32), V((rows, width), BF16), V((rows, hidden), BF16),
        V((rows, local), BF16), V((rows, 3 * local), BF16),
        V((6, 8, width), F32), V((8, hidden), F32), V((2, 8, local), F32),
        V((pairs, 8, width), F32),
        V((3, pairs, seq, width), BF16), V((3, pairs, seq, width), BF16),
        *[V((6, *(2,) * n, chunk, part), BF16) for n in (4, 3, 2, 1, 0)],
        *[V((3, *(2,) * n, chunk, local), BF16) for n in (4, 3, 2, 1, 0)],
        *[V((*(2,) * n, chunk, split), BF16) for n in (4, 3, 2, 1, 0)],
        *[V((*(2,) * n, chunk, local - split), BF16) for n in (4, 3, 2, 1, 0)],
        *[V((*(2,) * n, SMALL_ROWS, LANES), F32) for n in (4, 3, 2, 1, 0)],
        V((8 * docs_dev, LANES), BF16), V((n_batch, 8 * docs_dev, LANES), BF16),
        V((n_batch, 8 * docs_dev, LANES), F32), V((n_batch, 8 * docs_dev, LANES), F32),
        V((pairs, 8, LANES), F32), V((pairs, 8, LANES), F32),
        dma((3, pairs, 2)), dma((3, pairs, 2)), dma((pairs, local // LANES)),
        dma((pairs, local // LANES)), dma((3,)), dma((3,)), dma((12, 4)), dma((12, 4)),
        dma((2, n_batch)), dma((2, n_batch)), dma((1,)), dma((1,)), dma((25,)),
    ]
    shape = jax.ShapeDtypeStruct
    mixed, tokens_grad, grads, small, docs = pl.pallas_call(
        functools.partial(layer_kernel, (n_batch, pairs, seq)),
        out_shape=(
            V((rows, width), BF16),
            V((rows, width), BF16),
            V((3, chunk, hidden), F32),
            V((SMALL_ROWS, LANES), F32),
            V((8 * docs_dev, LANES), F32),
        ),
        in_specs=[hbm] * 19,
        out_specs=(vmem,) * 5,
        scratch_shapes=scratch,
        compiler_params=pltpu.CompilerParams(
            collective_id=0, has_side_effects=True, vmem_limit_bytes=60 * 1024 * 1024
        ),
        name="encoder_layer",
    )(
        tokens, cotangent, w_query, w_key, w_value, w_out, w_inner, w_outer,
        doc_vectors, doc_ids, *smalls,
    )

    inner = n_batch // GROUP
    if inner > 1:
        groups = [[g * inner + i for i in range(inner)] for g in range(GROUP)]
        grads = lax.psum_scatter(
            grads, "batch", scatter_dimension=1, axis_index_groups=groups, tiled=True
        )
        small = lax.psum(small, "batch", axis_index_groups=groups)
        part = lax.axis_index("batch") % inner
        pieces = []
        for row in range(SMALL_ROWS):
            wide = {ROW_BQ: local, ROW_BV: local, ROW_BIN: hidden}.get(row, width)
            size = wide // n_batch
            piece = lax.dynamic_slice(small[row], (part * size,), (size,))
            pieces.append(jnp.pad(piece, (0, LANES - size)))
        small = jnp.stack(pieces)

    if inner == 1:
        mixed, tokens_grad, grads, small, docs = (
            pltpu.with_memory_space_constraint(item, pltpu.VMEM)
            for item in (mixed, tokens_grad, grads, small, docs)
        )
    out_rows = width // n_batch
    vector = shape((out_rows,), F32)
    vector_local = shape((local // n_batch,), F32)
    square = shape((out_rows, local), F32)
    (
        mixed, tokens_grad, doc_grad, wq_grad, bq_grad, wk_grad, wv_grad, bv_grad, wo_grad, bo_grad, g1_grad, s1_grad,
        wi_grad, bi_grad, w2_grad, b2_grad, g2_grad, s2_grad,
    ) = pl.pallas_call(
        functools.partial(finish_kernel, local),
        out_shape=(
            shape((rows, width), BF16), shape((rows, width), BF16),
            shape((docs_dev, width), F32), square, vector_local, square, square, vector_local,
            square, vector, vector, vector,
            shape((out_rows, hidden), F32), shape((hidden // n_batch,), F32),
            shape((out_rows, hidden), F32), vector, vector, vector,
        ),
        in_specs=[vmem] * 5,
        out_specs=(
            hbm, hbm, vmem, hbm, vmem, hbm, hbm, vmem, hbm, vmem, vmem, vmem, hbm, vmem, hbm,
            vmem, vmem, vmem,
        ),
        scratch_shapes=[dma((8,))],
        name="gradient_outputs",
    )(mixed, tokens_grad, grads, small, docs)
    return (
        mixed, tokens_grad, doc_grad, wq_grad, bq_grad, wk_grad, wv_grad, bv_grad, wo_grad.T,
        bo_grad, g1_grad, s1_grad, wi_grad, bi_grad, w2_grad.T, b2_grad, g2_grad, s2_grad,
    )


def solution(mesh):
    in_specs = (
        P("batch", None), P("batch", None), P("batch"), P(None, "tensor"), P("tensor"),
        P(None, "tensor"), P(None, "tensor"), P("tensor"), P("tensor", None), P(), P(), P(),
        P(None, "tensor"), P("tensor"), P("tensor", None), P(), P(), P(), P("batch", None),
    )
    out_specs = (
        P("batch", None), P("batch", None), P("batch", None), P("batch", "tensor"),
        P(("tensor", "batch")), P("batch", "tensor"), P("batch", "tensor"),
        P(("tensor", "batch")), P("tensor", "batch"), P("batch"), P("batch"), P("batch"),
        P("batch", "tensor"), P(("tensor", "batch")), P("tensor", "batch"), P("batch"),
        P("batch"), P("batch"),
    )
    return jax.shard_map(
        functools.partial(body, mesh.shape["batch"]),
        mesh=mesh, in_specs=in_specs, out_specs=out_specs, check_vma=False,
    )
```
